32 devices in a mesh: shard: 4 (over z), ctx: 2 (over x), tp: 4 (over y, core).
Axes of the slice: x: 2, y: 2, z: 4, core: 2. Of those that a mesh axis runs over, the one named last changes fastest.
Arguments:
- tokens: bfloat16 [16, 1536, 960], P(('shard', 'tp'), 'ctx'), may hold values from -6 to 6
- span_ids: int32 [4], replicated, may hold values from 0 to 3, each once
- w_query: bfloat16 [2, 960, 960], P(None, ('shard', 'ctx')), may hold values from -0.1875 to 0.1875
- key_weight: bfloat16 [2, 960, 320], P(None, ('shard', 'ctx')), may hold values from -0.1875 to 0.1875
- value_weight: bfloat16 [2, 960, 320], P(None, ('shard', 'ctx')), may hold values from -0.1875 to 0.1875
- w_out: bfloat16 [2, 960, 960], P(None, None, ('shard', 'ctx')), may hold values from -2.5 to 2.5
- gain_attn: bfloat16 [2, 960], P(None, ('shard', 'ctx')), may hold values from 0.099609375 to 1.8984375
- gain_mlp: bfloat16 [2, 960], P(None, ('shard', 'ctx')), may hold values from 0.099609375 to 1.8984375
- w_gate: bfloat16 [2, 960, 2560], P(None, ('shard', 'ctx'), 'tp'), may hold values from -0.1875 to 0.1875
- w_up: bfloat16 [2, 960, 2560], P(None, ('shard', 'ctx'), 'tp'), may hold values from -0.1875 to 0.1875
- w_down: bfloat16 [2, 2560, 960], P(None, 'tp', ('shard', 'ctx')), may hold values from -0.125 to 0.125
- out_grad: bfloat16 [16, 1536, 960], P(('shard', 'tp'), 'ctx'), may hold values from -6 to 6
Outputs:
- block_out: bfloat16 [16, 1536, 960], P(('shard', 'tp'), 'ctx')
- tokens_grad: float32 [16, 1536, 960], P(('shard', 'tp'), 'ctx')
- grad_query: float32 [2, 960, 960], P(None, ('shard', 'ctx'))
- grad_key: float32 [2, 960, 320], P(None, ('shard', 'ctx'))
- grad_value: float32 [2, 960, 320], P(None, ('shard', 'ctx'))
- grad_out: float32 [2, 960, 960], P(None, None, ('shard', 'ctx'))
- grad_gain_attn: float32 [2, 960], P(None, ('shard', 'ctx'))
- grad_gain_mlp: float32 [2, 960], P(None, ('shard', 'ctx'))
- grad_gate: float32 [2, 960, 2560], P(None, ('shard', 'ctx'), 'tp')
- grad_up: float32 [2, 960, 2560], P(None, ('shard', 'ctx'), 'tp')
- grad_down: float32 [2, 2560, 960], P(None, 'tp', ('shard', 'ctx'))
The draws below stay inside these ranges and needn't reach their ends.
Inputs may be any that keep to these rules, and one draw needn't show every extreme that they name: a permutation; stored row j of every sequence is its token at position span_ids[j // c] * c + j % c with c = 1536 // (2 * 2).
All inputs are finite; a program needn't handle non-finite values.
Results may differ from the reference program's by a relative error of at most 0.033.
Values may be sent and summed in bfloat16 or wider, within the bound.
No kernel may reach another device: no remote copies, remote signals or barrier semaphores. Data moves between devices by JAX's collectives and lax.ppermute only.
A program may use at most 512 MiB of HBM per device.

```python
import jax
import jax.numpy as jnp
from jax import lax

MODEL_DIM = 960
QUERY_HEADS = 15
KEY_VALUE_HEADS = 5
HEAD_DIM = 64
FF = 2560
DECODER_LAYERS = 2
LENGTH = 1536
SEQS = 16
N_CTX = 2


def levels(stream_key, dims, shards, least, top_value):
    def one(position, blocks):
        steps = jax.random.uniform(jax.random.fold_in(jax.random.fold_in(stream_key, 6), position), (blocks,), jnp.float32, least / len(shards), top_value / len(shards))
        return jnp.repeat(jnp.exp(steps), dims[position] // blocks).reshape((-1,) + (1,) * (len(dims) - position - 1))

    gain = one(*shards[0])
    for cut in shards[1:]:
        gain = gain * one(*cut)
    return gain


def scatter_about(stream_key, shape, scale, bound, shards=(), kind=jnp.bfloat16):
    values = jax.random.normal(stream_key, shape, jnp.float32) * scale
    if len(shards) > 0:
        values = levels(stream_key, shape, shards, -0.22, 0.18) * values
    return jnp.clip(values, min=-bound, max=bound).astype(kind)


def setup_inputs(seed: int = 0) -> dict:
    arg_keys = jax.random.split(jax.random.key(seed), 13)
    return {
        "tokens": scatter_about(arg_keys[0], (SEQS, LENGTH, MODEL_DIM), 1.0, 6.0, ((0, 16), (1, 2))),
        "span_ids": jax.random.permutation(arg_keys[1], 2 * N_CTX).astype(jnp.int32),
        "w_query": scatter_about(arg_keys[2], (DECODER_LAYERS, MODEL_DIM, QUERY_HEADS * HEAD_DIM), MODEL_DIM ** -0.5, 0.1875, ((1, 8),)),
        "key_weight": scatter_about(arg_keys[3], (DECODER_LAYERS, MODEL_DIM, KEY_VALUE_HEADS * HEAD_DIM), MODEL_DIM ** -0.5, 0.1875, ((1, 8),)),
        "value_weight": scatter_about(arg_keys[4], (DECODER_LAYERS, MODEL_DIM, KEY_VALUE_HEADS * HEAD_DIM), MODEL_DIM ** -0.5, 0.1875, ((1, 8),)),
        "w_out": scatter_about(arg_keys[5], (DECODER_LAYERS, QUERY_HEADS * HEAD_DIM, MODEL_DIM), (QUERY_HEADS * HEAD_DIM * 8 // LENGTH) ** -0.5, 2.5, ((2, 8),)),
        "gain_attn": jnp.clip(1.0 + 0.18 * jax.random.normal(arg_keys[6], (DECODER_LAYERS, MODEL_DIM), jnp.float32), 0.099609375, 1.8984375).astype(jnp.bfloat16),
        "gain_mlp": jnp.clip(1.0 + 0.18 * jax.random.normal(arg_keys[7], (DECODER_LAYERS, MODEL_DIM), jnp.float32), 0.099609375, 1.8984375).astype(jnp.bfloat16),
        "w_gate": scatter_about(arg_keys[8], (DECODER_LAYERS, MODEL_DIM, FF), MODEL_DIM ** -0.5, 0.1875, ((1, 8), (2, 4))),
        "w_up": scatter_about(arg_keys[9], (DECODER_LAYERS, MODEL_DIM, FF), MODEL_DIM ** -0.5, 0.1875, ((1, 8), (2, 4))),
        "w_down": scatter_about(arg_keys[10], (DECODER_LAYERS, FF, MODEL_DIM), FF ** -0.5, 0.125, ((1, 4), (2, 8))),
        "out_grad": scatter_about(arg_keys[11], (SEQS, LENGTH, MODEL_DIM), 1.0, 6.0, ((0, 16), (1, 2))),
    }


EPS = 1e-05
THETA = 10000.0
MASKED = -1e+30

@jax.custom_vjp
def reduced_precision(v):
    return lax.optimization_barrier(v.astype(jnp.bfloat16)).astype(jnp.float32)

@jax.custom_vjp
def reduced_precision_back(v):
    return v

def low_keep(v):
    return (reduced_precision(v), None)

def low_pass(kept, grad):
    return (grad,)

def back_keep(v):
    return (v, None)

def back_low(kept, grad):
    return (reduced_precision(grad),)
reduced_precision.defvjp(low_keep, low_pass)
reduced_precision_back.defvjp(back_keep, back_low)

def matrix_product_exact(left, right):
    return jnp.dot(left, right, precision=lax.Precision.HIGHEST)

def rms_norm(hidden, gain_f):
    return hidden * lax.rsqrt(lax.optimization_barrier(jnp.mean(hidden * hidden, axis=-1, keepdims=True)) + EPS) * gain_f

def apply_rotation(values, cosine_table, sine_table):
    middle = values.shape[-1] // 2
    turned = jnp.concatenate([-values[..., middle:], values[..., :middle]], axis=-1)
    return values * cosine_table[:, None, :] + turned * sine_table[:, None, :]

def one_layer(hidden, weights, cosine_table, sine_table, causal):
    w_query, key_weight, value_weight, w_out, gain_a, gain_m, w_gate, w_up, w_down = weights
    sequence_length = hidden.shape[0]
    attention_input = reduced_precision(rms_norm(hidden, gain_a))
    query_rows = reduced_precision(apply_rotation(reduced_precision_back(matrix_product_exact(attention_input, w_query)).reshape(sequence_length, QUERY_HEADS, HEAD_DIM), cosine_table, sine_table))
    key_matrix = reduced_precision(apply_rotation(reduced_precision_back(matrix_product_exact(attention_input, key_weight)).reshape(sequence_length, KEY_VALUE_HEADS, HEAD_DIM), cosine_table, sine_table))
    value_matrix = reduced_precision(reduced_precision_back(matrix_product_exact(attention_input, value_weight))).reshape(sequence_length, KEY_VALUE_HEADS, HEAD_DIM)
    grouped_keys = query_rows.reshape(sequence_length, KEY_VALUE_HEADS, QUERY_HEADS // KEY_VALUE_HEADS, HEAD_DIM)
    scores = jnp.einsum('qkgd,tkd->kgqt', grouped_keys, key_matrix, precision=lax.Precision.HIGHEST) * HEAD_DIM ** (-0.5)
    scores = jnp.where(causal, reduced_precision_back(scores), MASKED)
    attn_prob = reduced_precision(jax.nn.softmax(scores, axis=-1))
    mixed = jnp.einsum('kgqt,tkd->qkgd', attn_prob, value_matrix, precision=lax.Precision.HIGHEST)
    mixed = reduced_precision(reduced_precision_back(mixed.reshape(sequence_length, QUERY_HEADS * HEAD_DIM)))
    hidden_mid = hidden + reduced_precision_back(matrix_product_exact(mixed, w_out))
    mlp_in = reduced_precision(rms_norm(hidden_mid, gain_m))
    gate_val = reduced_precision_back(matrix_product_exact(mlp_in, w_gate))
    up_val = reduced_precision_back(matrix_product_exact(mlp_in, w_up))
    inner_act = reduced_precision(jax.nn.silu(gate_val) * up_val)
    return hidden_mid + reduced_precision_back(matrix_product_exact(inner_act, w_down))

def reference(tokens, span_ids, w_query, key_weight, value_weight, w_out, gain_attn, gain_mlp, w_gate, w_up, w_down, out_grad):
    span_len = LENGTH // (2 * N_CTX)
    slot_ids = jnp.arange(LENGTH, dtype=jnp.int32)
    positions = span_ids[slot_ids // span_len] * span_len + slot_ids % span_len
    causal = positions[None, :] <= positions[:, None]
    inverse_freq = THETA ** (-jnp.arange(HEAD_DIM // 2, dtype=jnp.float32) * 2.0 / HEAD_DIM)
    angles = positions.astype(jnp.float32)[:, None] * inverse_freq[None, :]
    angles = jnp.concatenate([angles, angles], axis=-1)
    cosine_table = jnp.cos(angles)
    sine_table = jnp.sin(angles)
    params = tuple((weight_arr.astype(jnp.float32) for weight_arr in (w_query, key_weight, value_weight, w_out, gain_attn, gain_mlp, w_gate, w_up, w_down)))

    def whole_block(hidden, *weights):
        for layer_idx in range(DECODER_LAYERS):
            hidden = one_layer(hidden, [weight_arr[layer_idx] for weight_arr in weights], cosine_table, sine_table, causal)
        return hidden

    def seq_step(running, seq_pair):
        seq_in, seq_grad = seq_pair
        result, pullback = jax.vjp(whole_block, seq_in.astype(jnp.float32), *params)
        gradients = pullback(seq_grad.astype(jnp.float32))
        running = tuple((acc + part for acc, part in zip(running, gradients[1:])))
        return (running, (result.astype(jnp.bfloat16), gradients[0]))
    zero_sums = tuple((jnp.zeros_like(weight_arr) for weight_arr in params))
    totals, (outputs, in_grads) = lax.scan(seq_step, zero_sums, (tokens, out_grad))
    return (outputs, in_grads, totals[0], totals[1], totals[2], totals[3], totals[4], totals[5], totals[6], totals[7], totals[8])
```

```python
import functools

import jax
import jax.numpy as jnp
from jax import lax
from jax.experimental import pallas as pl
from jax.experimental.pallas import tpu as pltpu
from jax.sharding import PartitionSpec as P

QUERY_HEADS = 15
KEY_VALUE_HEADS = 5
GROUP = QUERY_HEADS // KEY_VALUE_HEADS
HEAD_DIM = 64
DECODER_LAYERS = 2
WIDE = 1024

EPS = 1e-05
THETA = 10000.0
MASKED = -1e30
LOG2E = 1.4426950408889634
SCALE = HEAD_DIM**-0.5
BF = jnp.bfloat16
F32 = jnp.float32
VMEM_LIMIT = 60 * 1024 * 1024

NN = (((1,), (0,)), ((), ()))
NT = (((1,), (1,)), ((), ()))
TN = (((0,), (0,)), ((), ()))


def mm(left, right, dims=NN):
    return lax.dot_general(left, right, dims, preferred_element_type=F32)


CORE_SWAP = [(0, 1), (1, 0), (2, 3), (3, 2)]
PAIR_SWAP = [(0, 2), (2, 0), (1, 3), (3, 1)]


def pick(array, index, axis):
    return lax.dynamic_index_in_dim(array, index, axis, keepdims=False)


def line_reduce(array, axis, name):
    count = array.shape[axis]
    rank = lax.axis_index(name)
    total = pick(array, rank, axis).astype(F32)
    for shift in range(1, count):
        sent = pick(array, (rank + shift) % count, axis)
        total += lax.ppermute(
            sent, name, [(i, (i + shift) % count) for i in range(count)]
        ).astype(F32)
    return total.astype(BF)


def pair_reduce(array, axis):
    pair = lax.axis_index("tp") // 2
    return pick(array, pair, axis) + lax.ppermute(pick(array, 1 - pair, axis), "tp", PAIR_SWAP)


class Reduction:
    def __init__(self, there, here, n_shard, n_ctx, rows):
        self.shape = (2, n_shard, n_ctx, rows, there.shape[-1])
        self.stage = 0
        self.values = (there.reshape(self.shape), here.reshape(self.shape))

    def advance(self):
        self.stage += 1
        if self.stage == 1:
            there, here = self.values
            self.values = (here, lax.ppermute(there, "tp", CORE_SWAP))
        elif self.stage == 2:
            here, came = self.values
            half = self.shape[1] // 2
            first = here[:, :half] + came[:, :half]
            second = here[:, half:] + came[:, half:]
            self.values = (pair_reduce(first, 0), line_reduce(second, 2, "ctx"))
        elif self.stage == 3:
            first, second = self.values
            self.values = (line_reduce(first, 1, "ctx"), pair_reduce(second, 0))
        elif self.stage == 4:
            self.values = (line_reduce(jnp.concatenate(self.values, axis=0), 0, "shard"),)
        return self.values


def gather_pair(array):
    pair = lax.axis_index("tp") // 2
    far = lax.ppermute(array, "tp", PAIR_SWAP)
    return jnp.stack([jnp.where(pair == 0, array, far), jnp.where(pair == 0, far, array)])


def gather_core(array, axis):
    core = lax.axis_index("tp") % 2
    far = lax.ppermute(array, "tp", CORE_SWAP)
    return jnp.stack([jnp.where(core == 0, array, far), jnp.where(core == 0, far, array)], axis=axis)


def gather_line(array, name, axis):
    count = lax.axis_size(name)
    rank = lax.axis_index(name)
    pieces = jnp.stack(
        [array]
        + [
            lax.ppermute(array, name, [(i, (i + shift) % count) for i in range(count)])
            for shift in range(1, count)
        ]
    )
    return jnp.stack([pick(pieces, (rank - j) % count, 0) for j in range(count)], axis=axis)


class Gathering:
    def __init__(self, share):
        self.stage = 0
        self.values = (share,)

    def advance(self):
        self.stage += 1
        if self.stage == 1:
            pieces = gather_line(self.values[0], "shard", 0)
            half = pieces.shape[1] // 2
            self.values = (pieces[:, :half], pieces[:, half:])
        elif self.stage == 2:
            first, second = self.values
            self.values = (gather_line(first, "ctx", 1), gather_pair(second))
        elif self.stage == 3:
            first, second = self.values
            self.values = (gather_pair(first), gather_line(second, "ctx", 2))
        elif self.stage == 4:
            joined = gather_core(jnp.concatenate(self.values, axis=3), 1)
            self.values = (joined.reshape(4, WIDE, joined.shape[-1]),)
        return self.values


def call(kernel, grid, in_specs, out_specs, out_shape, scratch, flops, moved, operands, after=(), scalars=()):
    used = len(scalars) + len(operands)

    def body(*refs):
        kernel(*refs[:used], *refs[used + len(after) :])

    return pl.pallas_call(
        body,
        grid_spec=pltpu.PrefetchScalarGridSpec(
            num_scalar_prefetch=len(scalars),
            grid=grid,
            in_specs=list(in_specs) + [pl.BlockSpec(memory_space=pl.ANY)] * len(after),
            out_specs=out_specs,
            scratch_shapes=scratch,
        ),
        out_shape=out_shape,
        compiler_params=pltpu.CompilerParams(vmem_limit_bytes=VMEM_LIMIT),
        cost_estimate=pl.CostEstimate(flops=flops, bytes_accessed=moved, transcendentals=0),
    )(*scalars, *operands, *after)


def full(*shape):
    return pl.BlockSpec(shape, lambda *at: (0,) * len(shape))


def row_steps(rows):
    step = 256 if rows % 256 == 0 else rows
    return [pl.ds(at, step) for at in range(0, rows, step)]


def mlp_forward_kernel(normed_ref, mid_ref, gate_w, up_w, down_w, out_ref, gate_ref, up_ref):
    @pl.when(pl.program_id(0) == 0)
    def _():
        out_ref[...] = mid_ref[...]

    for part in row_steps(normed_ref.shape[0]):
        normed = normed_ref[part, :]
        gate = mm(normed, gate_w[0])
        up = mm(normed, up_w[0])
        gate_ref[0, part, :] = gate
        up_ref[0, part, :] = up
        inner = (gate * jax.nn.sigmoid(gate) * up).astype(BF)
        out_ref[part, :] += mm(inner, down_w[0], NT)


def weight_specs(columns):
    return [
        pl.BlockSpec((1, WIDE, columns), functools.partial(lambda c, t: (t, 0, c), c))
        for c in range(3)
    ]


def mlp_forward(normed, mid, weights, after=()):
    rows = normed.shape[0]
    columns = weights.shape[2] // 3
    parts = weights.shape[0]
    whole = pl.BlockSpec((rows, WIDE), lambda t: (0, 0))
    kept = pl.BlockSpec((1, rows, columns), lambda t: (t, 0, 0))
    return call(
        mlp_forward_kernel,
        (parts,),
        [whole, whole] + weight_specs(columns),
        [whole, kept, kept],
        [
            jax.ShapeDtypeStruct((rows, WIDE), F32),
            jax.ShapeDtypeStruct((parts, rows, columns), F32),
            jax.ShapeDtypeStruct((parts, rows, columns), F32),
        ],
        [],
        6 * rows * WIDE * columns * parts,
        weights.size * 2 + rows * (WIDE * 10 + columns * parts * 8),
        (normed, mid, weights, weights, weights),
        after,
    )


def mlp_backward_kernel(
    order_ref,
    grad_ref,
    normed_ref,
    base_ref,
    gate_ref,
    up_ref,
    gate_w,
    up_w,
    down_w,
    back_ref,
    out_w,
    inner,
    gate_g,
    up_g,
):
    @pl.when(pl.program_id(0) == 0)
    def _():
        back_ref[...] = base_ref[...]

    columns = gate_ref.shape[2]
    for part in row_steps(grad_ref.shape[0]):
        act_grad = mm(grad_ref[part, :], down_w[0])
        gate = gate_ref[0, part, :]
        up = up_ref[0, part, :]
        sig = jax.nn.sigmoid(gate)
        silu = gate * sig
        inner[part, :] = (silu * up).astype(BF)
        gate_part = (act_grad * up * sig * (1.0 + gate * (1.0 - sig))).astype(BF)
        up_part = (act_grad * silu).astype(BF)
        gate_g[part, :] = gate_part
        up_g[part, :] = up_part
        back_ref[part, :] += mm(gate_part, gate_w[0], NT) + mm(up_part, up_w[0], NT)
    for at in range(0, WIDE, 256):
        part = pl.ds(at, 256)
        normed = normed_ref[:, part]
        out_w[0, part, 0:columns] = mm(normed, gate_g[...], TN).astype(BF)
        out_w[0, part, columns : 2 * columns] = mm(normed, up_g[...], TN).astype(BF)
        out_w[0, part, 2 * columns : 3 * columns] = mm(grad_ref[:, part], inner[...], TN).astype(BF)


def mlp_backward(order, grad, normed, base, gate, up, weights, after=()):
    rows = normed.shape[0]
    columns = weights.shape[2] // 3
    parts = order.shape[0]
    whole = full(rows, WIDE)
    kept = pl.BlockSpec((1, rows, columns), lambda i, order: (order[i], 0, 0))
    weight_parts = [
        pl.BlockSpec((1, WIDE, columns), functools.partial(lambda c, i, order: (order[i], 0, c), c))
        for c in range(3)
    ]
    return call(
        mlp_backward_kernel,
        (parts,),
        [whole, whole, whole, kept, kept] + weight_parts,
        [whole, pl.BlockSpec((1, WIDE, 3 * columns), lambda i, order: (i, 0, 0))],
        [
            jax.ShapeDtypeStruct((rows, WIDE), F32),
            jax.ShapeDtypeStruct((parts, WIDE, 3 * columns), BF),
        ],
        [pltpu.VMEM((rows, columns), BF)] * 3,
        12 * rows * WIDE * columns * parts,
        parts * WIDE * columns * 12 + rows * (WIDE * 12 + columns * parts * 8),
        (grad, normed, base, gate, up, weights, weights, weights),
        after,
        (order,),
    )


def turn_pairs(values):
    lane = lax.broadcasted_iota(jnp.int32, values.shape, 1) % HEAD_DIM
    return jnp.where(
        lane < HEAD_DIM // 2, -pltpu.roll(values, 96, 1), pltpu.roll(values, 32, 1)
    )


def low_lanes(values):
    lane = lax.broadcasted_iota(jnp.int32, values.shape, 1)
    return jnp.where(lane < HEAD_DIM, values, jnp.zeros_like(values))


def high_lanes(values):
    lane = lax.broadcasted_iota(jnp.int32, values.shape, 1)
    return jnp.where(lane < HEAD_DIM, jnp.zeros_like(values), values)


def other_half(values):
    return jnp.concatenate([values[:, HEAD_DIM:], values[:, :HEAD_DIM]], axis=1)


def row_scale(hidden, width):
    return lax.rsqrt(jnp.sum(hidden * hidden, axis=-1, keepdims=True) / width + EPS)


def project_kernel(width, hidden_ref, gain_ref, weights_ref, cos_ref, sin_ref, normed_ref, query_ref, pair_ref):
    for rows in row_steps(hidden_ref.shape[0]):
        hidden = hidden_ref[rows, :]
        normed = (hidden * row_scale(hidden, width) * gain_ref[...]).astype(BF)
        normed_ref[rows, :] = normed
        cosine, sine = cos_ref[rows, :], sin_ref[rows, :]
        keys = []
        for part in range(3):
            block = mm(normed, weights_ref[part] if part < 2 else weights_ref[part, :, :384])
            for at in range(5 if part < 2 else 3):
                two = block[:, at * 128 : at * 128 + 128]
                if part < 2:
                    two = two * cosine + turn_pairs(two) * sine
                two = two.astype(BF)
                for side in range(2):
                    head = part * 10 + at * 2 + side
                    if head < QUERY_HEADS:
                        query_ref[head, rows, :] = low_lanes(other_half(two) if side else two)
                    elif head < QUERY_HEADS + KEY_VALUE_HEADS:
                        keys.append(low_lanes(other_half(two) if side else two))
                    elif head < QUERY_HEADS + 2 * KEY_VALUE_HEADS:
                        group = head - QUERY_HEADS - KEY_VALUE_HEADS
                        pair_ref[group, rows, :] = keys[group] + high_lanes(two if side else other_half(two))


def project(hidden, gain, weights, cosine, sine, width, after=()):
    rows = hidden.shape[0]
    return call(
        functools.partial(project_kernel, width),
        (1,),
        [full(rows, WIDE), full(1, WIDE), full(3, WIDE, 640), full(rows, 128), full(rows, 128)],
        [full(rows, WIDE), full(QUERY_HEADS, rows, 128), full(KEY_VALUE_HEADS, rows, 128)],
        [
            jax.ShapeDtypeStruct((rows, WIDE), BF),
            jax.ShapeDtypeStruct((QUERY_HEADS, rows, 128), BF),
            jax.ShapeDtypeStruct((KEY_VALUE_HEADS, rows, 128), BF),
        ],
        [],
        2 * rows * WIDE * 1600,
        WIDE * 1600 * 2 + rows * WIDE * 6 + rows * 128 * 48,
        (hidden, gain, weights, cosine, sine),
        after,
    )


def join_heads(heads):
    columns = [heads[0]]
    for at in range(1, len(heads), 2):
        columns.append(other_half(heads[at]) + heads[at + 1])
    return columns


def out_forward_kernel(width, mixed_ref, weights_ref, hidden_ref, gain_ref, first_ref, last_ref, mid_ref, normed_ref):
    for rows in row_steps(hidden_ref.shape[0]):
        heads = [mixed_ref[head, rows, :] for head in range(QUERY_HEADS)]
        blank = jnp.zeros_like(heads[0])
        first = jnp.concatenate([blank, blank] + join_heads(heads[:5]), axis=1)
        pairs = [other_half(heads[at]) + heads[at + 1] for at in range(5, QUERY_HEADS, 2)]
        last = jnp.concatenate(pairs, axis=1)
        first_ref[rows, :] = first
        last_ref[rows, :] = last
        mid = hidden_ref[rows, :] + mm(first, weights_ref[0], NT) + mm(last, weights_ref[1], NT)
        mid_ref[rows, :] = mid
        normed_ref[rows, :] = (mid * row_scale(mid, width) * gain_ref[...]).astype(BF)


def out_forward(mixed, weights, hidden, gain, width, after=()):
    rows = hidden.shape[0]
    return call(
        functools.partial(out_forward_kernel, width),
        (1,),
        [
            full(QUERY_HEADS, rows, 128),
            pl.BlockSpec((2, WIDE, 640), lambda i: (1, 0, 0)),
            full(rows, WIDE),
            full(1, WIDE),
        ],
        [full(rows, 640), full(rows, 640), full(rows, WIDE), full(rows, WIDE)],
        [
            jax.ShapeDtypeStruct((rows, 640), BF),
            jax.ShapeDtypeStruct((rows, 640), BF),
            jax.ShapeDtypeStruct((rows, WIDE), F32),
            jax.ShapeDtypeStruct((rows, WIDE), BF),
        ],
        [],
        4 * rows * WIDE * 640,
        WIDE * 640 * 4 + rows * WIDE * 10 + rows * 6400,
        (mixed, weights, hidden, gain),
        after,
    )


def norm_back(gradient, hidden, gain, width):
    scaling = row_scale(hidden, width)
    normed = hidden * scaling
    weighted = gradient * gain
    inner = jnp.sum(weighted * normed, axis=-1, keepdims=True) / width
    gain_grad = jnp.sum(gradient * normed, axis=0, keepdims=True)
    return scaling * (weighted - normed * inner), gain_grad


def out_backward_kernel(
    width, back_ref, mid_ref, grad_ref, gain_ref, weights_ref, mid_g, rounded_ref, mixed_g, gain_g
):
    gain_g[...] = jnp.zeros_like(gain_g)
    for rows in row_steps(mid_ref.shape[0]):
        change, gain_part = norm_back(back_ref[rows, :], mid_ref[rows, :], gain_ref[...], width)
        gain_g[...] += gain_part
        change += grad_ref[rows, :]
        mid_g[rows, :] = change
        rounded = change.astype(BF)
        rounded_ref[rows, :] = rounded
        for part in range(2):
            block = mm(rounded, weights_ref[part]).astype(BF)
            for at in range(5):
                for side in range(2):
                    head = part * 10 + at * 2 + side - 5
                    if head >= 0:
                        two = block[:, at * 128 : at * 128 + 128]
                        mixed_g[head, rows, :] = high_lanes(two if side else other_half(two))


def out_backward(back, mid, grad, gain, weights, width, after=()):
    rows = mid.shape[0]
    return call(
        functools.partial(out_backward_kernel, width),
        (1,),
        [
            full(rows, WIDE),
            full(rows, WIDE),
            full(rows, WIDE),
            full(1, WIDE),
            pl.BlockSpec((2, WIDE, 640), lambda i: (1, 0, 0)),
        ],
        [full(rows, WIDE), full(rows, WIDE), full(QUERY_HEADS, rows, 128), full(1, WIDE)],
        [
            jax.ShapeDtypeStruct((rows, WIDE), F32),
            jax.ShapeDtypeStruct((rows, WIDE), BF),
            jax.ShapeDtypeStruct((QUERY_HEADS, rows, 128), BF),
            jax.ShapeDtypeStruct((1, WIDE), F32),
        ],
        [],
        4 * rows * WIDE * 640,
        WIDE * 640 * 4 + rows * WIDE * 18 + rows * 3840,
        (back, mid, grad, gain, weights),
        after,
    )


def outer_products(left, right):
    return [mm(left[:, at : at + 256], right, TN).astype(BF) for at in range(0, WIDE, 256)]


def query_backward_kernel(query_g, normed_ref, rounded_ref, last_ref, first_ref, out_w):
    for rows in row_steps(normed_ref.shape[0]):
        first_ref[rows, :] = jnp.concatenate(
            [query_g[at, rows, :] + other_half(query_g[at + 1, rows, :]) for at in range(0, 10, 2)], axis=1
        )
    for slot, left, right in ((0, normed_ref, first_ref), (1, rounded_ref, last_ref)):
        for at in range(0, WIDE, 256):
            out_w[slot, pl.ds(at, 256), :] = mm(left[:, pl.ds(at, 256)], right[...], TN).astype(BF)


def query_backward(query_g, normed, rounded, last, after=()):
    rows = normed.shape[0]
    return call(
        query_backward_kernel,
        (1,),
        [full(10, rows, 128), full(rows, WIDE), full(rows, WIDE), full(rows, 640)],
        [full(rows, 640), full(2, WIDE, 640)],
        [jax.ShapeDtypeStruct((rows, 640), BF), jax.ShapeDtypeStruct((2, WIDE, 640), BF)],
        [],
        4 * rows * WIDE * 640,
        WIDE * 640 * 4 + rows * WIDE * 4 + rows * 5120,
        (query_g, normed, rounded, last),
        after,
    )


def key_backward_kernel(
    width,
    shares,
    *refs,
):
    pairs = refs[:shares]
    query_g, first_ref, mixed_ref, normed_ref, rounded_ref, weights_ref, hidden_ref, mid_g, gain_ref = refs[shares : shares + 9]
    cos_ref, sin_ref, grad_ref, out_w, gain_g, second, third = refs[shares + 9 :]
    gain_g[...] = jnp.zeros_like(gain_g)
    for rows in row_steps(hidden_ref.shape[0]):
        keys, values = [], []
        for group in range(KEY_VALUE_HEADS):
            pair = pairs[0][group, rows, :]
            for other in pairs[1:]:
                pair = pair + other[group, rows, :].astype(F32)
            moved = pair * sin_ref[rows, :]
            lane = lax.broadcasted_iota(jnp.int32, pair.shape, 1)
            turned = jnp.where(lane < HEAD_DIM // 2, pltpu.roll(moved, 96, 1), -pltpu.roll(moved, 32, 1))
            key = pair * cos_ref[rows, :] + turned
            keys.append(low_lanes(key).astype(BF))
            values.append(high_lanes(pair).astype(BF))
        heads = [query_g[at, rows, :] for at in range(5)] + keys
        second_part = jnp.concatenate(
            [heads[at] + other_half(heads[at + 1]) for at in range(0, 10, 2)], axis=1
        )
        blank = jnp.zeros_like(values[0])
        third_part = jnp.concatenate(
            [
                other_half(values[0]) + values[1],
                other_half(values[2]) + values[3],
                other_half(values[4]),
                blank,
                blank,
            ],
            axis=1,
        )
        second[rows, :] = second_part
        third[rows, :] = third_part
        back = (
            mm(first_ref[rows, :], weights_ref[0], NT)
            + mm(second_part, weights_ref[1], NT)
            + mm(third_part, weights_ref[2], NT)
        )
        change, gain_part = norm_back(back, hidden_ref[rows, :], gain_ref[...], width)
        gain_g[...] += gain_part
        grad_ref[rows, :] = mid_g[rows, :] + change
    for at in range(0, WIDE, 256):
        part = pl.ds(at, 256)
        out_w[0, part, :] = mm(normed_ref[:, part], second[...], TN).astype(BF)
        out_w[1, part, :] = (
            mm(normed_ref[:, part], third[...], TN) + mm(rounded_ref[:, part], mixed_ref[...], TN)
        ).astype(BF)


def key_backward(
    pair_g, arrived, query_g, first, mixed, normed, rounded, weights, hidden, mid_g, gain, cosine, sine, width, after=()
):
    rows = hidden.shape[0]
    own = pl.BlockSpec((KEY_VALUE_HEADS, rows, 128), lambda i: (0, 0, 0))
    return call(
        functools.partial(key_backward_kernel, width, 1 + len(arrived)),
        (1,),
        [own] * (1 + len(arrived))
        + [
            pl.BlockSpec((5, rows, 128), lambda i: (2, 0, 0)),
            full(rows, 640),
            full(rows, 640),
            full(rows, WIDE),
            full(rows, WIDE),
            full(3, WIDE, 640),
            full(rows, WIDE),
            full(rows, WIDE),
            full(1, WIDE),
            full(rows, 128),
            full(rows, 128),
        ],
        [full(rows, WIDE), full(2, WIDE, 640), full(1, WIDE)],
        [
            jax.ShapeDtypeStruct((rows, WIDE), F32),
            jax.ShapeDtypeStruct((2, WIDE, 640), BF),
            jax.ShapeDtypeStruct((1, WIDE), F32),
        ],
        [pltpu.VMEM((rows, 640), BF)] * 2,
        12 * rows * WIDE * 640,
        WIDE * 640 * 10 + rows * WIDE * 16 + rows * 12800,
        (pair_g, *arrived, query_g, first, mixed, normed, rounded, weights, hidden, mid_g, gain, cosine, sine),
        after,
    )


def attend_kernel(ids_ref, query_ref, pair_ref, out_ref, total_ref, turned, top, norm, mixed):
    span = query_ref.shape[1] // 2
    spans = pair_ref.shape[1] // span
    width = GROUP * span
    for j in range(spans):
        values = pair_ref[0, j * span : (j + 1) * span, :].astype(F32)
        turned[:, j * span : (j + 1) * span] = values.T[HEAD_DIM:, :].astype(BF)
    key_at = lax.broadcasted_iota(jnp.int32, (span, span), 0)
    query_at = lax.broadcasted_iota(jnp.int32, (span, span), 1)
    bias = jnp.where(key_at <= query_at, 0.0, MASKED)
    bias = jnp.concatenate([bias] * GROUP, axis=1)
    for s in range(2):
        query = query_ref[:, s * span : (s + 1) * span, :].reshape(width, 128)

        def scores(j):
            return mm(pair_ref[0, j * span : (j + 1) * span, :], query, NT) * (SCALE * LOG2E)

        first = scores(s) + bias
        peak = jnp.max(first, axis=0, keepdims=True)
        weight = jnp.exp2(first - peak)
        top[...] = peak
        norm[...] = jnp.sum(weight, axis=0, keepdims=True)
        mixed[...] = mm(turned[:, s * span : (s + 1) * span], weight.astype(BF))
        for j in range(spans):
            if j == s:
                continue

            @pl.when(ids_ref[j] < ids_ref[s])
            def _():
                more = scores(j)
                old = top[...]
                peak = jnp.maximum(old, jnp.max(more, axis=0, keepdims=True))
                keep = jnp.exp2(old - peak)
                weight = jnp.exp2(more - peak)
                top[...] = peak
                norm[...] = norm[...] * keep + jnp.sum(weight, axis=0, keepdims=True)
                mixed[...] = mixed[...] * keep + mm(
                    turned[:, j * span : (j + 1) * span], weight.astype(BF)
                )

        total_ref[0, s] = top[...] + jnp.log2(norm[...])
        result = mixed[...] / norm[...]
        result = jnp.concatenate([jnp.zeros_like(result), result], axis=0).T.astype(BF)
        out_ref[:, s * span : (s + 1) * span, :] = result.reshape(GROUP, span, 128)


def attend(ids, query, pairs, after=()):
    rows = query.shape[1]
    keys = pairs.shape[1]
    width = GROUP * rows // 2
    heads = pl.BlockSpec((GROUP, rows, 128), lambda g, ids: (g, 0, 0))
    return call(
        attend_kernel,
        (KEY_VALUE_HEADS,),
        [heads, pl.BlockSpec((1, keys, 128), lambda g, ids: (g, 0, 0))],
        [heads, pl.BlockSpec((1, 2, 1, width), lambda g, ids: (g, 0, 0, 0))],
        [
            jax.ShapeDtypeStruct((QUERY_HEADS, rows, 128), BF),
            jax.ShapeDtypeStruct((KEY_VALUE_HEADS, 2, 1, width), F32),
        ],
        [
            pltpu.VMEM((HEAD_DIM, keys), BF),
            pltpu.VMEM((1, width), F32),
            pltpu.VMEM((1, width), F32),
            pltpu.VMEM((HEAD_DIM, width), F32),
        ],
        8 * QUERY_HEADS * rows * keys * 128,
        QUERY_HEADS * rows * 1024,
        (query, pairs),
        after,
        (ids,),
    )


def attend_back_kernel(
    ids_ref, query_ref, pair_ref, grad_ref, out_ref, total_ref, cos_ref, sin_ref, query_g, pair_g, turned, deltas, mixed
):
    span = query_ref.shape[1] // 2
    spans = pair_ref.shape[1] // span
    width = GROUP * span
    half = HEAD_DIM // 2
    for j in range(spans):
        values = pair_ref[0, j * span : (j + 1) * span, :].astype(F32)
        turned[:, j * span : (j + 1) * span] = values.T[:HEAD_DIM, :].astype(BF)
    pair_g[...] = jnp.zeros_like(pair_g)
    key_at = lax.broadcasted_iota(jnp.int32, (span, span), 0)
    query_at = lax.broadcasted_iota(jnp.int32, (span, span), 1)
    bias = jnp.where(key_at <= query_at, 0.0, MASKED)
    bias = jnp.concatenate([bias] * GROUP, axis=1)
    for s in range(2):
        own = slice(s * span, (s + 1) * span)
        query = query_ref[:, own, :].reshape(width, 128)
        grad = grad_ref[:, own, :].reshape(width, 128)
        product = grad.astype(F32) * out_ref[:, own, :].reshape(width, 128).astype(F32)
        deltas[...] = jnp.sum(product.T, axis=0, keepdims=True)

        def block(j, diagonal):
            at = slice(j * span, (j + 1) * span)
            pair = pair_ref[0, at, :]
            scores = mm(pair, query, NT) * (SCALE * LOG2E) - total_ref[0, s]
            if diagonal:
                scores = scores + bias
            weight = jnp.exp2(scores)
            change = (weight * (mm(pair, grad, NT) - deltas[...])).astype(BF)
            pair_g[0, at, :] += mm(change, query) * SCALE + mm(weight.astype(BF), grad)
            return mm(turned[:, at], change)

        mixed[...] = block(s, True)
        for j in range(spans):
            if j == s:
                continue

            @pl.when(ids_ref[j] < ids_ref[s])
            def _():
                mixed[...] += block(j, False)

        cosine = jnp.concatenate([cos_ref[:, own]] * GROUP, axis=1)
        sine = jnp.concatenate([sin_ref[:, own]] * GROUP, axis=1)
        change = mixed[...] * SCALE
        moved = change * sine
        change = change * cosine + jnp.concatenate([moved[half:], -moved[:half]], axis=0)
        change = jnp.concatenate([change, jnp.zeros_like(change)], axis=0).T.astype(BF)
        query_g[:, own, :] = change.reshape(GROUP, span, 128)


def attend_back(ids, query, pairs, grad, out, total, cosine_t, sine_t, after=()):
    rows = query.shape[1]
    keys = pairs.shape[1]
    width = GROUP * rows // 2
    heads = pl.BlockSpec((GROUP, rows, 128), lambda g, ids: (g, 0, 0))
    both = pl.BlockSpec((1, keys, 128), lambda g, ids: (g, 0, 0))
    return call(
        attend_back_kernel,
        (KEY_VALUE_HEADS,),
        [
            heads,
            both,
            heads,
            heads,
            pl.BlockSpec((1, 2, 1, width), lambda g, ids: (g, 0, 0, 0)),
            full(HEAD_DIM, rows),
            full(HEAD_DIM, rows),
        ],
        [heads, both],
        [
            jax.ShapeDtypeStruct((QUERY_HEADS, rows, 128), BF),
            jax.ShapeDtypeStruct((KEY_VALUE_HEADS, keys, 128), F32),
        ],
        [
            pltpu.VMEM((HEAD_DIM, keys), BF),
            pltpu.VMEM((1, width), F32),
            pltpu.VMEM((HEAD_DIM, width), F32),
        ],
        20 * QUERY_HEADS * rows * keys * 128,
        QUERY_HEADS * rows * 2048,
        (query, pairs, grad, out, total, cosine_t, sine_t),
        after,
        (ids,),
    )


def plain_scores(query, pairs, places, own):
    grouped = query[..., :HEAD_DIM].reshape(KEY_VALUE_HEADS, GROUP, -1, HEAD_DIM)
    scores = jnp.einsum("kgqd,ktd->kgqt", grouped, pairs[..., :HEAD_DIM], preferred_element_type=F32)
    return grouped, jnp.where(places[None, :] <= own[:, None], scores * SCALE, MASKED)


def plain_attend(places, query, pairs, after=()):
    rows = query.shape[1]
    _, scores = plain_scores(query, pairs, places, places[:rows])
    top = jnp.max(scores, axis=-1, keepdims=True)
    weight = jnp.exp(scores - top)
    norm = jnp.sum(weight, axis=-1, keepdims=True)
    mixed = jnp.einsum(
        "kgqt,ktd->kgqd", (weight / norm).astype(BF), pairs[..., HEAD_DIM:], preferred_element_type=F32
    )
    mixed = jnp.pad(mixed.reshape(QUERY_HEADS, rows, HEAD_DIM), ((0, 0), (0, 0), (HEAD_DIM, 0)))
    return mixed.astype(BF), top + jnp.log(norm)


def plain_attend_back(places, query, pairs, grad, out, total, cosine_t, sine_t, after=()):
    rows = query.shape[1]
    half = HEAD_DIM // 2
    grouped, scores = plain_scores(query, pairs, places, places[:rows])
    weight = jnp.exp(scores - total)
    grad = grad[..., HEAD_DIM:].reshape(grouped.shape)
    reach = jnp.einsum("kgqd,ktd->kgqt", grad, pairs[..., HEAD_DIM:], preferred_element_type=F32)
    change = (weight * (reach - jnp.sum(weight * reach, axis=-1, keepdims=True))).astype(BF)
    query_g = SCALE * jnp.einsum("kgqt,ktd->kgqd", change, pairs[..., :HEAD_DIM], preferred_element_type=F32)
    key_g = SCALE * jnp.einsum("kgqt,kgqd->ktd", change, grouped, preferred_element_type=F32)
    value_g = jnp.einsum("kgqt,kgqd->ktd", weight.astype(BF), grad, preferred_element_type=F32)
    moved = query_g * sine_t.T
    query_g = query_g * cosine_t.T + jnp.concatenate([moved[..., half:], -moved[..., :half]], axis=-1)
    query_g = jnp.pad(query_g.reshape(QUERY_HEADS, rows, HEAD_DIM), ((0, 0), (0, 0), (0, HEAD_DIM)))
    return query_g.astype(BF), jnp.concatenate([key_g, value_g], axis=-1)


def local(
    tokens,
    span_ids,
    w_query,
    key_weight,
    value_weight,
    w_out,
    gain_attn,
    gain_mlp,
    w_gate,
    w_up,
    w_down,
    out_grad,
):
    group_count, local_length, model_width = tokens.shape
    assert group_count == 1
    n_ctx = lax.axis_size("ctx")
    n_shard = lax.axis_size("shard")
    blocks = n_ctx * n_shard
    own_rows = model_width // blocks
    rows = WIDE // blocks
    extra = rows - own_rows
    tp_rank = lax.axis_index("tp")
    ctx_rank = lax.axis_index("ctx")
    span = local_length // 2

    ids = jnp.concatenate(
        [lax.dynamic_slice_in_dim(span_ids, 2 * ((ctx_rank - i) % n_ctx), 2) for i in range(n_ctx)]
    )
    places = (ids[:, None] * span + jnp.arange(span, dtype=jnp.int32)[None, :]).reshape(-1)
    own_place = places[:local_length].astype(F32)
    inverse_freq = THETA ** (-jnp.arange(HEAD_DIM // 2, dtype=F32) * 2.0 / HEAD_DIM)
    angles = own_place[:, None] * jnp.tile(inverse_freq, 4)[None, :]
    cosine, sine = jnp.cos(angles), jnp.sin(angles)
    angles_t = jnp.tile(inverse_freq, 2)[:, None] * own_place[None, :]
    cosine_t, sine_t = jnp.cos(angles_t), jnp.sin(angles_t)

    source = jnp.arange(model_width, dtype=jnp.int32)
    target = source // own_rows * rows + source % own_rows
    spread = (target[:, None] == jnp.arange(WIDE, dtype=jnp.int32)[None, :]).astype(BF)

    def attn_share(layer):
        joined = jnp.concatenate(
            [w_query[layer], key_weight[layer], value_weight[layer], w_out[layer].T], axis=1
        )
        share = lax.dynamic_slice_in_dim(joined, tp_rank * 640, 640, 1)
        gains = jnp.concatenate(
            [
                jnp.pad(gain_attn[layer], (0, 128 - own_rows)),
                jnp.pad(gain_mlp[layer], (0, 640 - 128 - own_rows)),
            ]
        )
        gains = jnp.where(tp_rank == 0, gains, jnp.zeros_like(gains))
        return jnp.concatenate([share, gains[None, :], jnp.zeros((extra - 1, 640), BF)], axis=0)

    def mlp_share(layer):
        joined = jnp.concatenate([w_gate[layer], w_up[layer], w_down[layer].T], axis=1)
        return jnp.pad(joined, ((0, extra), (0, 0)))

    def gather(share):
        return lax.all_gather(share, ("tp", "shard", "ctx"), axis=0, tiled=True).reshape(
            4, WIDE, share.shape[1]
        )

    def gains_of(weights):
        lines = weights[0].reshape(blocks, rows, 640)[:, own_rows, :]
        return tuple(
            lines[:, at : at + rows].reshape(WIDE).astype(F32)[None, :] for at in (0, 128)
        )

    use_kernels = span % 128 == 0
    if use_kernels:
        attend_call = functools.partial(attend, ids)
        attend_back_call = functools.partial(attend_back, ids)
    else:
        attend_call = functools.partial(plain_attend, places)
        attend_back_call = functools.partial(plain_attend_back, places)

    mlp_w = [gather(mlp_share(layer)) for layer in range(DECODER_LAYERS)]
    attn_now = Gathering(attn_share(0))
    for _ in range(4):
        attn_now.advance()

    hidden = mm(tokens[0], spread)
    kept = []
    for layer in range(DECODER_LAYERS):
        weights = attn_now.values[0]
        gain_a, gain_m = gains_of(weights)
        if layer + 1 < DECODER_LAYERS:
            attn_now = Gathering(attn_share(layer + 1))
            following = attn_now.advance
        else:
            following = tuple
        attn_in, query, pair = project(hidden, gain_a, weights, cosine, sine, model_width)
        ready = following()
        around = [pair]
        for shift in range(1, n_ctx):
            around.append(
                lax.ppermute(pair, "ctx", [(i, (i + shift) % n_ctx) for i in range(n_ctx)])
            )
        pairs = jnp.concatenate(around, axis=1)
        mixed, total = attend_call(query, pairs, after=ready)
        ready = following()
        first, last, mid, mlp_in = out_forward(mixed, weights, hidden, gain_m, model_width, after=ready)
        ready = following()
        result, gate, up = mlp_forward(mlp_in, mid, mlp_w[layer], after=ready)
        following()
        kept.append(
            (hidden, weights, gain_a, gain_m, attn_in, query, pairs, mixed, total, first, last, mid, mlp_in, gate, up)
        )
        hidden = result
    block_out = mm(hidden.astype(BF), spread, NT).astype(BF)[None]

    core = tp_rank % 2
    grad_run = mm(out_grad[0], spread)
    blank = jnp.zeros_like(grad_run)
    mlp_done, attn_done = [None] * DECODER_LAYERS, [None] * DECODER_LAYERS
    attn_sum = None
    for layer in reversed(range(DECODER_LAYERS)):
        (hidden, weights, gain_a, gain_m, attn_in, query, pairs, mixed, total, first, last, mid, mlp_in, gate, up) = kept[layer]
        attn_step = attn_sum.advance if attn_sum is not None else tuple
        grad_in = grad_run.astype(BF)
        sources = (gate, up, mlp_w[layer])
        mlp_step = tuple
        if layer > 0:
            back, parts = mlp_backward(jnp.arange(4, dtype=jnp.int32), grad_in, mlp_in, blank, *sources)
            summed = lax.psum_scatter(
                parts.reshape(4 * WIDE, -1), ("tp", "shard", "ctx"), scatter_dimension=0, tiled=True
            )
            mlp_done[layer] = summed
            ready = ()
        else:
            pair_at = jnp.array([0, 2], jnp.int32)
            ready = attn_step()
            back, there = mlp_backward(pair_at + 1 - core, grad_in, mlp_in, blank, *sources)
            ready = attn_step()
            back, here = mlp_backward(pair_at + core, grad_in, mlp_in, back, *sources, after=ready[:0])
            mlp_sum = Reduction(there, here, n_shard, n_ctx, rows)
            mlp_step = mlp_sum.advance
            mlp_step()
            ready = ready + mlp_sum.values[1:]
        mid_g, rounded, mixed_g, gain_m_grad = out_backward(
            back, mid, grad_run, gain_m, weights, model_width, after=ready
        )
        ready = attn_step()
        mlp_step()
        query_g, pair_g = attend_back_call(query, pairs, mixed_g, mixed, total, cosine_t, sine_t, after=ready)
        ready = attn_step() + (mlp_sum.values if layer == 0 else ())
        arrived = [
            lax.ppermute(
                pair_g[:, shift * local_length : (shift + 1) * local_length].astype(BF),
                "ctx",
                [(i, (i - shift) % n_ctx) for i in range(n_ctx)],
            )
            for shift in range(1, n_ctx)
        ]
        first_g, early = query_backward(query_g, attn_in, rounded, last, after=ready)
        mlp_step()
        if attn_sum is not None:
            attn_done[layer + 1] = gather_core(gather_pair(attn_sum.values[0]), 1)
        ready = mlp_sum.values if layer == 0 else ()
        grad_run, late, gain_a_grad = key_backward(
            pair_g,
            arrived,
            query_g,
            first_g,
            first,
            attn_in,
            rounded,
            weights,
            hidden,
            mid_g,
            gain_a,
            cosine,
            sine,
            model_width,
            after=ready,
        )
        mlp_step()
        lines = jnp.concatenate(
            [
                jnp.pad(gain_a_grad.reshape(blocks, rows), ((0, 0), (0, 128 - rows))),
                jnp.pad(gain_m_grad.reshape(blocks, rows), ((0, 0), (0, 640 - 128 - rows))),
            ],
            axis=1,
        ).astype(BF)
        at = lax.broadcasted_iota(jnp.int32, (1, rows, 1), 1)
        second_w = jnp.where(at == own_rows, lines[:, None, :], late[0].reshape(blocks, rows, 640))
        second_w = second_w.reshape(WIDE, 640)
        there = jnp.stack([jnp.where(core == 0, second_w, early[0]), jnp.where(core == 0, early[1], late[1])])
        here = jnp.stack([jnp.where(core == 0, early[0], second_w), jnp.where(core == 0, late[1], early[1])])
        attn_sum = Reduction(there, here, n_shard, n_ctx, rows)
    for _ in range(4):
        attn_sum.advance()
    attn_done[0] = gather_core(gather_pair(attn_sum.values[0]), 1)
    mlp_done[0] = mlp_sum.values[0]

    grad_high = grad_run.astype(BF)
    grad_low = (grad_run - grad_high.astype(F32)).astype(BF)
    tokens_grad = (mm(grad_high, spread, NT) + mm(grad_low, spread, NT))[None]

    outs = [[] for _ in range(9)]
    for mlp, attn in zip(mlp_done, attn_done):
        attn = attn.reshape(4, rows, 640)
        line = attn[1, own_rows].astype(F32)
        attn = attn[:, :own_rows].transpose(1, 0, 2).reshape(own_rows, 2560).astype(F32)
        mlp = mlp[:own_rows].astype(F32)
        columns = mlp.shape[1] // 3
        for slot, value in enumerate(
            (
                attn[:, :960],
                attn[:, 960:1280],
                attn[:, 1280:1600],
                attn[:, 1600:].T,
                line[:own_rows],
                line[128 : 128 + own_rows],
                mlp[:, :columns],
                mlp[:, columns : 2 * columns],
                mlp[:, 2 * columns :].T,
            )
        ):
            outs[slot].append(value)
    return (block_out, tokens_grad, *[jnp.stack(parts) for parts in outs])


def solution(mesh):
    return jax.shard_map(
        local,
        mesh=mesh,
        in_specs=(
            P(("shard", "tp"), "ctx", None),
            P(),
            P(None, ("shard", "ctx"), None),
            P(None, ("shard", "ctx"), None),
            P(None, ("shard", "ctx"), None),
            P(None, None, ("shard", "ctx")),
            P(None, ("shard", "ctx")),
            P(None, ("shard", "ctx")),
            P(None, ("shard", "ctx"), "tp"),
            P(None, ("shard", "ctx"), "tp"),
            P(None, "tp", ("shard", "ctx")),
            P(("shard", "tp"), "ctx", None),
        ),
        out_specs=(
            P(("shard", "tp"), "ctx", None),
            P(("shard", "tp"), "ctx", None),
            P(None, ("shard", "ctx"), None),
            P(None, ("shard", "ctx"), None),
            P(None, ("shard", "ctx"), None),
            P(None, None, ("shard", "ctx")),
            P(None, ("shard", "ctx")),
            P(None, ("shard", "ctx")),
            P(None, ("shard", "ctx"), "tp"),
            P(None, ("shard", "ctx"), "tp"),
            P(None, "tp", ("shard", "ctx")),
        ),
        check_vma=False,
    )
```

```python
import functools

import jax
import jax.numpy as jnp
from jax import lax
from jax.experimental import pallas as pl
from jax.experimental.pallas import tpu as pltpu
from jax.sharding import PartitionSpec as P

QUERY_HEADS = 15
KEY_VALUE_HEADS = 5
GROUP = QUERY_HEADS // KEY_VALUE_HEADS
HEAD_DIM = 64
DECODER_LAYERS = 2
WIDE = 1024

EPS = 1e-05
THETA = 10000.0
MASKED = -1e30
LOG2E = 1.4426950408889634
SCALE = HEAD_DIM**-0.5
BF = jnp.bfloat16
F32 = jnp.float32
VMEM_LIMIT = 60 * 1024 * 1024

NN = (((1,), (0,)), ((), ()))
NT = (((1,), (1,)), ((), ()))
TN = (((0,), (0,)), ((), ()))


def mm(left, right, dims=NN):
    return lax.dot_general(left, right, dims, preferred_element_type=F32)


CORE_SWAP = [(0, 1), (1, 0), (2, 3), (3, 2)]
PAIR_SWAP = [(0, 2), (2, 0), (1, 3), (3, 1)]


def pick(array, index, axis):
    return lax.dynamic_index_in_dim(array, index, axis, keepdims=False)


def pick_sum(arrays, index, axis):
    total = pick(arrays[0], index, axis)
    for array in arrays[1:]:
        total = total + pick(array, index, axis)
    return total


def tips(arrays):
    return tuple(array[(0,) * (array.ndim - 2)][:8, :128] for array in arrays)


def line_reduce(arrays, axis, name, start=0):
    count = arrays[0].shape[axis]
    rank = lax.axis_index(name)
    total = pick_sum(arrays, rank, axis).astype(F32)
    for shift in range(1, count):
        sent = pick_sum(arrays, (rank + shift) % count + start, axis)
        total += lax.ppermute(
            sent, name, [(i, (i + shift) % count) for i in range(count)]
        ).astype(F32)
    return total.astype(BF)


def pair_reduce(arrays, axis, start=0):
    pair = lax.axis_index("tp") // 2
    sent = lax.ppermute(pick_sum(arrays, 1 - pair + start, axis), "tp", PAIR_SWAP)
    return pick_sum(arrays, pair, axis) + sent


class Reduction:
    def __init__(self, there, here, n_shard, n_ctx, rows):
        self.shape = (2, n_shard // 2, n_ctx, rows, there[0].shape[-1])
        self.stage = 0
        self.values = (there, here)

    def advance(self, start=0):
        self.stage += 1
        if self.stage == 1:
            there, here = self.values
            came = tuple(lax.ppermute(part, "tp", CORE_SWAP) for part in there)
            self.values = came + tuple(here)
        elif self.stage == 2:
            parts = [part.reshape(self.shape) for part in self.values]
            self.values = (
                pair_reduce(parts[0::2], 0, start),
                line_reduce(parts[1::2], 2, "ctx", start),
            )
        elif self.stage == 3:
            first, second = self.values
            self.values = (
                line_reduce([first], 1, "ctx", start),
                pair_reduce([second], 0, start),
            )
        elif self.stage == 4:
            joined = jnp.concatenate(self.values, axis=0)
            self.values = (line_reduce([joined], 0, "shard", start),)
        return self.values


def gather_pair(array):
    pair = lax.axis_index("tp") // 2
    far = lax.ppermute(array, "tp", PAIR_SWAP)
    return jnp.stack([jnp.where(pair == 0, array, far), jnp.where(pair == 0, far, array)])


def gather_core(array, axis):
    core = lax.axis_index("tp") % 2
    far = lax.ppermute(array, "tp", CORE_SWAP)
    return jnp.stack([jnp.where(core == 0, array, far), jnp.where(core == 0, far, array)], axis=axis)


def call(kernel, grid, in_specs, out_specs, out_shape, scratch, flops, moved, operands, after=(), scalars=()):
    used = len(scalars) + len(operands)
    outs = len(out_shape)

    def body(*refs):
        kept = refs[used + len(after) :]
        kept[outs][0] = 0
        kernel(*refs[:used], *kept[:outs], *kept[outs + 1 :])

    return pl.pallas_call(
        body,
        grid_spec=pltpu.PrefetchScalarGridSpec(
            num_scalar_prefetch=len(scalars),
            grid=grid,
            in_specs=list(in_specs) + [pl.BlockSpec(memory_space=pl.ANY)] * len(after),
            out_specs=list(out_specs) + [pl.BlockSpec(memory_space=pltpu.SMEM)],
            scratch_shapes=scratch,
        ),
        out_shape=list(out_shape) + [jax.ShapeDtypeStruct((1,), jnp.int32)],
        compiler_params=pltpu.CompilerParams(vmem_limit_bytes=VMEM_LIMIT),
        cost_estimate=pl.CostEstimate(flops=flops, bytes_accessed=moved, transcendentals=0),
    )(*scalars, *operands, *after)


def full(*shape):
    return pl.BlockSpec(shape, lambda *at: (0,) * len(shape))


def row_steps(rows):
    step = 256 if rows % 256 == 0 else rows
    return [pl.ds(at, step) for at in range(0, rows, step)]


def mlp_forward_kernel(normed_ref, mid_ref, gate_w, up_w, down_w, out_ref, gate_ref, up_ref):
    @pl.when(pl.program_id(0) == 0)
    def _():
        out_ref[...] = mid_ref[...]

    for part in row_steps(normed_ref.shape[0]):
        normed = normed_ref[part, :]
        gate = mm(normed, gate_w[0])
        up = mm(normed, up_w[0])
        gate_ref[0, part, :] = gate
        up_ref[0, part, :] = up
        inner = (gate * jax.nn.sigmoid(gate) * up).astype(BF)
        out_ref[part, :] += mm(inner, down_w[0], NT)


def mlp_forward(normed, mid, weights, start, columns, after=()):
    rows = normed.shape[0]
    parts = weights.shape[0]
    whole = full(rows, WIDE)
    kept = pl.BlockSpec((1, rows, columns), lambda t: (t, 0, 0))
    return call(
        mlp_forward_kernel,
        (parts,),
        [whole, whole]
        + [
            pl.BlockSpec((1, WIDE, columns), functools.partial(lambda c, t: (t, 0, c), start + c))
            for c in range(3)
        ],
        [whole, kept, kept],
        [
            jax.ShapeDtypeStruct((rows, WIDE), F32),
            jax.ShapeDtypeStruct((parts, rows, columns), F32),
            jax.ShapeDtypeStruct((parts, rows, columns), F32),
        ],
        [],
        6 * rows * WIDE * columns * parts,
        WIDE * columns * parts * 6 + rows * (WIDE * 10 + columns * parts * 8),
        (normed, mid, weights, weights, weights),
        after,
    )


def mlp_backward_kernel(
    order_ref,
    grad_ref,
    normed_ref,
    base_ref,
    gate_ref,
    up_ref,
    gate_w,
    up_w,
    down_w,
    back_ref,
    *rest,
):
    *outs, inner, gate_g, up_g = rest
    @pl.when(pl.program_id(0) == 0)
    def _():
        back_ref[...] = base_ref[...]

    columns = gate_ref.shape[2]
    for part in row_steps(grad_ref.shape[0]):
        act_grad = mm(grad_ref[part, :], down_w[0])
        gate = gate_ref[0, part, :]
        up = up_ref[0, part, :]
        sig = jax.nn.sigmoid(gate)
        silu = gate * sig
        inner[part, :] = (silu * up).astype(BF)
        gate_part = (act_grad * up * sig * (1.0 + gate * (1.0 - sig))).astype(BF)
        up_part = (act_grad * silu).astype(BF)
        gate_g[part, :] = gate_part
        up_g[part, :] = up_part
        back_ref[part, :] += mm(gate_part, gate_w[0], NT) + mm(up_part, up_w[0], NT)
    for at in range(0, WIDE, 256):
        part = pl.ds(at, 256)
        normed = normed_ref[:, part]
        out_w = outs[at * len(outs) // WIDE]
        part = pl.ds(at % (WIDE // len(outs)), 256)
        out_w[0, part, 0:columns] = mm(normed, gate_g[...], TN).astype(BF)
        out_w[0, part, columns : 2 * columns] = mm(normed, up_g[...], TN).astype(BF)
        out_w[0, part, 2 * columns : 3 * columns] = mm(grad_ref[:, pl.ds(at, 256)], inner[...], TN).astype(BF)


def mlp_backward(order, pieces, grad, normed, base, gate, up, weights, start, after=()):
    rows, columns = gate.shape[1:]
    parts = order.shape[0]
    whole = full(rows, WIDE)
    kept = pl.BlockSpec((1, rows, columns), lambda i, order: (order[i], 0, 0))
    weight_parts = [
        pl.BlockSpec((1, WIDE, columns), functools.partial(lambda c, i, order: (order[i], 0, c), start + c))
        for c in range(3)
    ]
    return call(
        mlp_backward_kernel,
        (parts,),
        [whole, whole, whole, kept, kept] + weight_parts,
        [whole] + [pl.BlockSpec((1, WIDE // pieces, 3 * columns), lambda i, order: (i, 0, 0))] * pieces,
        [jax.ShapeDtypeStruct((rows, WIDE), F32)]
        + [jax.ShapeDtypeStruct((parts, WIDE // pieces, 3 * columns), BF)] * pieces,
        [pltpu.VMEM((rows, columns), BF)] * 3,
        12 * rows * WIDE * columns * parts,
        parts * WIDE * columns * 12 + rows * (WIDE * 12 + columns * parts * 8),
        (grad, normed, base, gate, up, weights, weights, weights),
        after,
        (order,),
    )


def turn_pairs(values):
    lane = lax.broadcasted_iota(jnp.int32, values.shape, 1) % HEAD_DIM
    return jnp.where(
        lane < HEAD_DIM // 2, -pltpu.roll(values, 96, 1), pltpu.roll(values, 32, 1)
    )


def low_lanes(values):
    lane = lax.broadcasted_iota(jnp.int32, values.shape, 1)
    return jnp.where(lane < HEAD_DIM, values, jnp.zeros_like(values))


def high_lanes(values):
    lane = lax.broadcasted_iota(jnp.int32, values.shape, 1)
    return jnp.where(lane < HEAD_DIM, jnp.zeros_like(values), values)


def other_half(values):
    return jnp.concatenate([values[:, HEAD_DIM:], values[:, :HEAD_DIM]], axis=1)


def row_scale(hidden, width):
    return lax.rsqrt(jnp.sum(hidden * hidden, axis=-1, keepdims=True) / width + EPS)


def project_kernel(width, hidden_ref, gain_ref, weights_ref, cos_ref, sin_ref, normed_ref, query_ref, pair_ref):
    for rows in row_steps(hidden_ref.shape[0]):
        hidden = hidden_ref[rows, :]
        normed = (hidden * row_scale(hidden, width) * gain_ref[...]).astype(BF)
        normed_ref[rows, :] = normed
        cosine, sine = cos_ref[rows, :], sin_ref[rows, :]
        keys = []
        for part in range(3):
            block = mm(normed, weights_ref[part] if part < 2 else weights_ref[part, :, :384])
            for at in range(5 if part < 2 else 3):
                two = block[:, at * 128 : at * 128 + 128]
                if part < 2:
                    two = two * cosine + turn_pairs(two) * sine
                two = two.astype(BF)
                for side in range(2):
                    head = part * 10 + at * 2 + side
                    if head < QUERY_HEADS:
                        query_ref[head, rows, :] = low_lanes(other_half(two) if side else two)
                    elif head < QUERY_HEADS + KEY_VALUE_HEADS:
                        keys.append(low_lanes(other_half(two) if side else two))
                    elif head < QUERY_HEADS + 2 * KEY_VALUE_HEADS:
                        group = head - QUERY_HEADS - KEY_VALUE_HEADS
                        pair_ref[group, rows, :] = keys[group] + high_lanes(two if side else other_half(two))


def project(hidden, gain, weights, layer, cosine, sine, width, after=()):
    rows = hidden.shape[0]
    return call(
        functools.partial(project_kernel, width),
        (1,),
        [
            full(rows, WIDE),
            full(1, WIDE),
            pl.BlockSpec((3, WIDE, 640), lambda i: (0, 0, layer)),
            full(rows, 128),
            full(rows, 128),
        ],
        [full(rows, WIDE), full(QUERY_HEADS, rows, 128), full(KEY_VALUE_HEADS, rows, 128)],
        [
            jax.ShapeDtypeStruct((rows, WIDE), BF),
            jax.ShapeDtypeStruct((QUERY_HEADS, rows, 128), BF),
            jax.ShapeDtypeStruct((KEY_VALUE_HEADS, rows, 128), BF),
        ],
        [],
        2 * rows * WIDE * 1600,
        WIDE * 1600 * 2 + rows * WIDE * 6 + rows * 128 * 48,
        (hidden, gain, weights, cosine, sine),
        after,
    )


def join_heads(heads):
    columns = [heads[0]]
    for at in range(1, len(heads), 2):
        columns.append(other_half(heads[at]) + heads[at + 1])
    return columns


def out_forward_kernel(width, mixed_ref, weights_ref, hidden_ref, gain_ref, first_ref, last_ref, mid_ref, normed_ref):
    for rows in row_steps(hidden_ref.shape[0]):
        heads = [mixed_ref[head, rows, :] for head in range(QUERY_HEADS)]
        blank = jnp.zeros_like(heads[0])
        first = jnp.concatenate([blank, blank] + join_heads(heads[:5]), axis=1)
        pairs = [other_half(heads[at]) + heads[at + 1] for at in range(5, QUERY_HEADS, 2)]
        last = jnp.concatenate(pairs, axis=1)
        first_ref[rows, :] = first
        last_ref[rows, :] = last
        mid = hidden_ref[rows, :] + mm(first, weights_ref[0], NT) + mm(last, weights_ref[1], NT)
        mid_ref[rows, :] = mid
        normed_ref[rows, :] = (mid * row_scale(mid, width) * gain_ref[...]).astype(BF)


def out_forward(mixed, weights, layer, hidden, gain, width, after=()):
    rows = hidden.shape[0]
    return call(
        functools.partial(out_forward_kernel, width),
        (1,),
        [
            full(QUERY_HEADS, rows, 128),
            pl.BlockSpec((2, WIDE, 640), lambda i: (1, 0, layer)),
            full(rows, WIDE),
            full(1, WIDE),
        ],
        [full(rows, 640), full(rows, 640), full(rows, WIDE), full(rows, WIDE)],
        [
            jax.ShapeDtypeStruct((rows, 640), BF),
            jax.ShapeDtypeStruct((rows, 640), BF),
            jax.ShapeDtypeStruct((rows, WIDE), F32),
            jax.ShapeDtypeStruct((rows, WIDE), BF),
        ],
        [],
        4 * rows * WIDE * 640,
        WIDE * 640 * 4 + rows * WIDE * 10 + rows * 6400,
        (mixed, weights, hidden, gain),
        after,
    )


def norm_back(gradient, hidden, gain, width):
    scaling = row_scale(hidden, width)
    normed = hidden * scaling
    weighted = gradient * gain
    inner = jnp.sum(weighted * normed, axis=-1, keepdims=True) / width
    gain_grad = jnp.sum(gradient * normed, axis=0, keepdims=True)
    return scaling * (weighted - normed * inner), gain_grad


def out_backward_kernel(
    width, back_ref, mid_ref, grad_ref, gain_ref, weights_ref, mid_g, rounded_ref, mixed_g, gain_g
):
    gain_g[...] = jnp.zeros_like(gain_g)
    for rows in row_steps(mid_ref.shape[0]):
        change, gain_part = norm_back(back_ref[rows, :], mid_ref[rows, :], gain_ref[...], width)
        gain_g[...] += gain_part
        change += grad_ref[rows, :]
        mid_g[rows, :] = change
        rounded = change.astype(BF)
        rounded_ref[rows, :] = rounded
        for part in range(2):
            block = mm(rounded, weights_ref[part]).astype(BF)
            for at in range(5):
                for side in range(2):
                    head = part * 10 + at * 2 + side - 5
                    if head >= 0:
                        two = block[:, at * 128 : at * 128 + 128]
                        mixed_g[head, rows, :] = high_lanes(two if side else other_half(two))


def out_backward(back, mid, grad, gain, weights, layer, width, after=()):
    rows = mid.shape[0]
    return call(
        functools.partial(out_backward_kernel, width),
        (1,),
        [
            full(rows, WIDE),
            full(rows, WIDE),
            full(rows, WIDE),
            full(1, WIDE),
            pl.BlockSpec((2, WIDE, 640), lambda i: (1, 0, layer)),
        ],
        [full(rows, WIDE), full(rows, WIDE), full(QUERY_HEADS, rows, 128), full(1, WIDE)],
        [
            jax.ShapeDtypeStruct((rows, WIDE), F32),
            jax.ShapeDtypeStruct((rows, WIDE), BF),
            jax.ShapeDtypeStruct((QUERY_HEADS, rows, 128), BF),
            jax.ShapeDtypeStruct((1, WIDE), F32),
        ],
        [],
        4 * rows * WIDE * 640,
        WIDE * 640 * 4 + rows * WIDE * 18 + rows * 3840,
        (back, mid, grad, gain, weights),
        after,
    )


def query_backward_kernel(
    query_g, normed_ref, rounded_ref, mixed_ref, last_ref, weights_ref, back_ref, out_w, mixed_w, first
):
    for rows in row_steps(normed_ref.shape[0]):
        part = jnp.concatenate(
            [query_g[at, rows, :] + other_half(query_g[at + 1, rows, :]) for at in range(0, 10, 2)], axis=1
        )
        first[rows, :] = part
        back_ref[rows, :] = mm(part, weights_ref[0], NT)
    for at in range(0, WIDE, 256):
        part = pl.ds(at, 256)
        out_w[0, part, :] = mm(normed_ref[:, part], first[...], TN).astype(BF)
        rounded = rounded_ref[:, part]
        out_w[1, part, :] = mm(rounded, last_ref[...], TN).astype(BF)
        mixed_w[part, :] = mm(rounded, mixed_ref[...], TN)


def query_backward(query_g, normed, rounded, mixed, last, weights, layer, after=()):
    rows = normed.shape[0]
    return call(
        query_backward_kernel,
        (1,),
        [
            full(10, rows, 128),
            full(rows, WIDE),
            full(rows, WIDE),
            full(rows, 640),
            full(rows, 640),
            pl.BlockSpec((1, WIDE, 640), lambda i: (0, 0, layer)),
        ],
        [full(rows, WIDE), full(2, WIDE, 640), full(WIDE, 640)],
        [
            jax.ShapeDtypeStruct((rows, WIDE), F32),
            jax.ShapeDtypeStruct((2, WIDE, 640), BF),
            jax.ShapeDtypeStruct((WIDE, 640), F32),
        ],
        [pltpu.VMEM((rows, 640), BF)],
        8 * rows * WIDE * 640,
        WIDE * 640 * 10 + rows * WIDE * 8 + rows * 5120,
        (query_g, normed, rounded, mixed, last, weights),
        after,
    )


def key_backward_kernel(width, shares, *refs):
    pairs = refs[:shares]
    query_g, back_ref, mixed_w, normed_ref, weights_ref, hidden_ref, mid_g, gain_ref = refs[shares : shares + 8]
    cos_ref, sin_ref, grad_ref, rounded_ref, out_w, gain_g, second, third = refs[shares + 8 :]
    gain_g[...] = jnp.zeros_like(gain_g)
    for rows in row_steps(hidden_ref.shape[0]):
        keys, values = [], []
        for group in range(KEY_VALUE_HEADS):
            pair = pairs[0][group, rows, :]
            for other in pairs[1:]:
                pair = pair + other[group, rows, :].astype(F32)
            moved = pair * sin_ref[rows, :]
            lane = lax.broadcasted_iota(jnp.int32, pair.shape, 1)
            turned = jnp.where(lane < HEAD_DIM // 2, pltpu.roll(moved, 96, 1), -pltpu.roll(moved, 32, 1))
            key = pair * cos_ref[rows, :] + turned
            keys.append(low_lanes(key).astype(BF))
            values.append(high_lanes(pair).astype(BF))
        heads = [query_g[at, rows, :] for at in range(5)] + keys
        second_part = jnp.concatenate(
            [heads[at] + other_half(heads[at + 1]) for at in range(0, 10, 2)], axis=1
        )
        third_part = jnp.concatenate(
            [other_half(values[0]) + values[1], other_half(values[2]) + values[3], other_half(values[4])],
            axis=1,
        )
        second[rows, :] = second_part
        third[rows, :] = third_part
        back = (
            back_ref[rows, :]
            + mm(second_part, weights_ref[1], NT)
            + mm(third_part, weights_ref[2, :, :384], NT)
        )
        change, gain_part = norm_back(back, hidden_ref[rows, :], gain_ref[...], width)
        gain_g[...] += gain_part
        grad = mid_g[rows, :] + change
        grad_ref[rows, :] = grad
        rounded_ref[rows, :] = grad.astype(BF)
    for at in range(0, WIDE, 256):
        part = pl.ds(at, 256)
        normed = normed_ref[:, part]
        out_w[0, part, :] = mm(normed, second[...], TN).astype(BF)
        out_w[1, part, :384] = (mm(normed, third[...], TN) + mixed_w[part, :384]).astype(BF)
        out_w[1, part, 384:] = mixed_w[part, 384:].astype(BF)


def key_backward(
    pair_g, arrived, query_g, back, mixed_w, normed, weights, layer, hidden, mid_g, gain, cosine, sine, width, after=()
):
    rows = hidden.shape[0]
    own = pl.BlockSpec((KEY_VALUE_HEADS, rows, 128), lambda i: (0, 0, 0))
    return call(
        functools.partial(key_backward_kernel, width, 1 + len(arrived)),
        (1,),
        [own] * (1 + len(arrived))
        + [
            pl.BlockSpec((5, rows, 128), lambda i: (2, 0, 0)),
            full(rows, WIDE),
            full(WIDE, 640),
            full(rows, WIDE),
            pl.BlockSpec((3, WIDE, 640), lambda i: (0, 0, layer)),
            full(rows, WIDE),
            full(rows, WIDE),
            full(1, WIDE),
            full(rows, 128),
            full(rows, 128),
        ],
        [full(rows, WIDE), full(rows, WIDE), full(2, WIDE, 640), full(1, WIDE)],
        [
            jax.ShapeDtypeStruct((rows, WIDE), F32),
            jax.ShapeDtypeStruct((rows, WIDE), BF),
            jax.ShapeDtypeStruct((2, WIDE, 640), BF),
            jax.ShapeDtypeStruct((1, WIDE), F32),
        ],
        [pltpu.VMEM((rows, 640), BF), pltpu.VMEM((rows, 384), BF)],
        7 * rows * WIDE * 640,
        WIDE * 640 * 12 + rows * WIDE * 20 + rows * 12800,
        (pair_g, *arrived, query_g, back, mixed_w, normed, weights, hidden, mid_g, gain, cosine, sine),
        after,
    )


def attend_kernel(ids_ref, query_ref, pair_ref, out_ref, total_ref, turned, top, norm, mixed):
    span = query_ref.shape[1] // 2
    spans = pair_ref.shape[1] // span
    width = GROUP * span
    for j in range(spans):
        values = pair_ref[0, j * span : (j + 1) * span, :].astype(F32)
        turned[:, j * span : (j + 1) * span] = values.T[HEAD_DIM:, :].astype(BF)
    key_at = lax.broadcasted_iota(jnp.int32, (span, span), 0)
    query_at = lax.broadcasted_iota(jnp.int32, (span, span), 1)
    bias = jnp.where(key_at <= query_at, 0.0, MASKED)
    bias = jnp.concatenate([bias] * GROUP, axis=1)
    for s in range(2):
        query = query_ref[:, s * span : (s + 1) * span, :].reshape(width, 128)

        def scores(j):
            return mm(pair_ref[0, j * span : (j + 1) * span, :], query, NT) * (SCALE * LOG2E)

        first = scores(s) + bias
        peak = jnp.max(first, axis=0, keepdims=True)
        weight = jnp.exp2(first - peak)
        top[...] = peak
        norm[...] = jnp.sum(weight, axis=0, keepdims=True)
        mixed[...] = mm(turned[:, s * span : (s + 1) * span], weight.astype(BF))
        for j in range(spans):
            if j == s:
                continue

            @pl.when(ids_ref[j] < ids_ref[s])
            def _():
                more = scores(j)
                old = top[...]
                peak = jnp.maximum(old, jnp.max(more, axis=0, keepdims=True))
                keep = jnp.exp2(old - peak)
                weight = jnp.exp2(more - peak)
                top[...] = peak
                norm[...] = norm[...] * keep + jnp.sum(weight, axis=0, keepdims=True)
                mixed[...] = mixed[...] * keep + mm(
                    turned[:, j * span : (j + 1) * span], weight.astype(BF)
                )

        total_ref[0, s] = top[...] + jnp.log2(norm[...])
        result = mixed[...] / norm[...]
        result = jnp.concatenate([jnp.zeros_like(result), result], axis=0).T.astype(BF)
        out_ref[:, s * span : (s + 1) * span, :] = result.reshape(GROUP, span, 128)


def attend(ids, query, pairs, after=()):
    rows = query.shape[1]
    keys = pairs.shape[1]
    width = GROUP * rows // 2
    heads = pl.BlockSpec((GROUP, rows, 128), lambda g, ids: (g, 0, 0))
    return call(
        attend_kernel,
        (KEY_VALUE_HEADS,),
        [heads, pl.BlockSpec((1, keys, 128), lambda g, ids: (g, 0, 0))],
        [heads, pl.BlockSpec((1, 2, 1, width), lambda g, ids: (g, 0, 0, 0))],
        [
            jax.ShapeDtypeStruct((QUERY_HEADS, rows, 128), BF),
            jax.ShapeDtypeStruct((KEY_VALUE_HEADS, 2, 1, width), F32),
        ],
        [
            pltpu.VMEM((HEAD_DIM, keys), BF),
            pltpu.VMEM((1, width), F32),
            pltpu.VMEM((1, width), F32),
            pltpu.VMEM((HEAD_DIM, width), F32),
        ],
        8 * QUERY_HEADS * rows * keys * 128,
        QUERY_HEADS * rows * 1024,
        (query, pairs),
        after,
        (ids,),
    )


def attend_back_kernel(
    ids_ref, query_ref, pair_ref, grad_ref, out_ref, total_ref, cos_ref, sin_ref, query_g, pair_g, turned, deltas, mixed
):
    span = query_ref.shape[1] // 2
    spans = pair_ref.shape[1] // span
    width = GROUP * span
    half = HEAD_DIM // 2
    for j in range(spans):
        values = pair_ref[0, j * span : (j + 1) * span, :].astype(F32)
        turned[:, j * span : (j + 1) * span] = values.T[:HEAD_DIM, :].astype(BF)
    pair_g[...] = jnp.zeros_like(pair_g)
    key_at = lax.broadcasted_iota(jnp.int32, (span, span), 0)
    query_at = lax.broadcasted_iota(jnp.int32, (span, span), 1)
    bias = jnp.where(key_at <= query_at, 0.0, MASKED)
    bias = jnp.concatenate([bias] * GROUP, axis=1)
    for s in range(2):
        own = slice(s * span, (s + 1) * span)
        query = query_ref[:, own, :].reshape(width, 128)
        grad = grad_ref[:, own, :].reshape(width, 128)
        product = grad.astype(F32) * out_ref[:, own, :].reshape(width, 128).astype(F32)
        deltas[...] = jnp.sum(product.T, axis=0, keepdims=True)

        def block(j, diagonal):
            at = slice(j * span, (j + 1) * span)
            pair = pair_ref[0, at, :]
            scores = mm(pair, query, NT) * (SCALE * LOG2E) - total_ref[0, s]
            if diagonal:
                scores = scores + bias
            weight = jnp.exp2(scores)
            change = (weight * (mm(pair, grad, NT) - deltas[...])).astype(BF)
            pair_g[0, at, :] += mm(change, query) * SCALE + mm(weight.astype(BF), grad)
            return mm(turned[:, at], change)

        mixed[...] = block(s, True)
        for j in range(spans):
            if j == s:
                continue

            @pl.when(ids_ref[j] < ids_ref[s])
            def _():
                mixed[...] += block(j, False)

        cosine = jnp.concatenate([cos_ref[:, own]] * GROUP, axis=1)
        sine = jnp.concatenate([sin_ref[:, own]] * GROUP, axis=1)
        change = mixed[...] * SCALE
        moved = change * sine
        change = change * cosine + jnp.concatenate([moved[half:], -moved[:half]], axis=0)
        change = jnp.concatenate([change, jnp.zeros_like(change)], axis=0).T.astype(BF)
        query_g[:, own, :] = change.reshape(GROUP, span, 128)


def attend_back(ids, query, pairs, grad, out, total, cosine_t, sine_t, after=()):
    rows = query.shape[1]
    keys = pairs.shape[1]
    width = GROUP * rows // 2
    heads = pl.BlockSpec((GROUP, rows, 128), lambda g, ids: (g, 0, 0))
    both = pl.BlockSpec((1, keys, 128), lambda g, ids: (g, 0, 0))
    return call(
        attend_back_kernel,
        (KEY_VALUE_HEADS,),
        [
            heads,
            both,
            heads,
            heads,
            pl.BlockSpec((1, 2, 1, width), lambda g, ids: (g, 0, 0, 0)),
            full(HEAD_DIM, rows),
            full(HEAD_DIM, rows),
        ],
        [heads, both],
        [
            jax.ShapeDtypeStruct((QUERY_HEADS, rows, 128), BF),
            jax.ShapeDtypeStruct((KEY_VALUE_HEADS, keys, 128), F32),
        ],
        [
            pltpu.VMEM((HEAD_DIM, keys), BF),
            pltpu.VMEM((1, width), F32),
            pltpu.VMEM((HEAD_DIM, width), F32),
        ],
        20 * QUERY_HEADS * rows * keys * 128,
        QUERY_HEADS * rows * 2048,
        (query, pairs, grad, out, total, cosine_t, sine_t),
        after,
        (ids,),
    )


def plain_scores(query, pairs, places, own):
    grouped = query[..., :HEAD_DIM].reshape(KEY_VALUE_HEADS, GROUP, -1, HEAD_DIM)
    scores = jnp.einsum("kgqd,ktd->kgqt", grouped, pairs[..., :HEAD_DIM], preferred_element_type=F32)
    return grouped, jnp.where(places[None, :] <= own[:, None], scores * SCALE, MASKED)


def plain_attend(places, query, pairs, after=()):
    rows = query.shape[1]
    _, scores = plain_scores(query, pairs, places, places[:rows])
    top = jnp.max(scores, axis=-1, keepdims=True)
    weight = jnp.exp(scores - top)
    norm = jnp.sum(weight, axis=-1, keepdims=True)
    mixed = jnp.einsum(
        "kgqt,ktd->kgqd", (weight / norm).astype(BF), pairs[..., HEAD_DIM:], preferred_element_type=F32
    )
    mixed = jnp.pad(mixed.reshape(QUERY_HEADS, rows, HEAD_DIM), ((0, 0), (0, 0), (HEAD_DIM, 0)))
    return mixed.astype(BF), top + jnp.log(norm), jnp.zeros((1,), jnp.int32)


def plain_attend_back(places, query, pairs, grad, out, total, cosine_t, sine_t, after=()):
    rows = query.shape[1]
    half = HEAD_DIM // 2
    grouped, scores = plain_scores(query, pairs, places, places[:rows])
    weight = jnp.exp(scores - total)
    grad = grad[..., HEAD_DIM:].reshape(grouped.shape)
    reach = jnp.einsum("kgqd,ktd->kgqt", grad, pairs[..., HEAD_DIM:], preferred_element_type=F32)
    change = (weight * (reach - jnp.sum(weight * reach, axis=-1, keepdims=True))).astype(BF)
    query_g = SCALE * jnp.einsum("kgqt,ktd->kgqd", change, pairs[..., :HEAD_DIM], preferred_element_type=F32)
    key_g = SCALE * jnp.einsum("kgqt,kgqd->ktd", change, grouped, preferred_element_type=F32)
    value_g = jnp.einsum("kgqt,kgqd->ktd", weight.astype(BF), grad, preferred_element_type=F32)
    moved = query_g * sine_t.T
    query_g = query_g * cosine_t.T + jnp.concatenate([moved[..., half:], -moved[..., :half]], axis=-1)
    query_g = jnp.pad(query_g.reshape(QUERY_HEADS, rows, HEAD_DIM), ((0, 0), (0, 0), (0, HEAD_DIM)))
    return query_g.astype(BF), jnp.concatenate([key_g, value_g], axis=-1), jnp.zeros((1,), jnp.int32)


def local(
    tokens,
    span_ids,
    w_query,
    key_weight,
    value_weight,
    w_out,
    gain_attn,
    gain_mlp,
    w_gate,
    w_up,
    w_down,
    out_grad,
):
    group_count, local_length, model_width = tokens.shape
    assert group_count == 1
    n_ctx = lax.axis_size("ctx")
    n_shard = lax.axis_size("shard")
    blocks = n_ctx * n_shard
    own_rows = model_width // blocks
    rows = WIDE // blocks
    extra = rows - own_rows
    tp_rank = lax.axis_index("tp")
    ctx_rank = lax.axis_index("ctx")
    span = local_length // 2

    ids = jnp.concatenate(
        [lax.dynamic_slice_in_dim(span_ids, 2 * ((ctx_rank - i) % n_ctx), 2) for i in range(n_ctx)]
    )
    places = (ids[:, None] * span + jnp.arange(span, dtype=jnp.int32)[None, :]).reshape(-1)
    own_place = places[:local_length].astype(F32)
    inverse_freq = THETA ** (-jnp.arange(HEAD_DIM // 2, dtype=F32) * 2.0 / HEAD_DIM)
    angles = own_place[:, None] * jnp.tile(inverse_freq, 4)[None, :]
    cosine, sine = jnp.cos(angles), jnp.sin(angles)
    angles_t = jnp.tile(inverse_freq, 2)[:, None] * own_place[None, :]
    cosine_t, sine_t = jnp.cos(angles_t), jnp.sin(angles_t)

    source = jnp.arange(model_width, dtype=jnp.int32)
    target = source // own_rows * rows + source % own_rows
    spread = (target[:, None] == jnp.arange(WIDE, dtype=jnp.int32)[None, :]).astype(BF)

    def attn_share(layer):
        joined = jnp.concatenate(
            [w_query[layer], key_weight[layer], value_weight[layer], w_out[layer].T], axis=1
        )
        gains = jnp.concatenate(
            [
                jnp.pad(gain_attn[layer], (0, 128 - own_rows)),
                jnp.pad(gain_mlp[layer], (0, 2560 - 128 - own_rows)),
            ]
        )
        joined = jnp.concatenate([joined, gains[None, :], jnp.zeros((extra - 1, 2560), BF)], axis=0)
        return lax.dynamic_slice_in_dim(joined, tp_rank * 640, 640, 1)

    def mlp_share(layer):
        joined = jnp.concatenate([w_gate[layer], w_up[layer], w_down[layer].T], axis=1)
        return jnp.pad(joined, ((0, extra), (0, 0)))

    def gather(share):
        return lax.all_gather(share, ("tp", "shard", "ctx"), axis=0, tiled=True).reshape(
            4, WIDE, share.shape[1]
        )


    def gains_of(weights, layer):
        lines = weights[0, :, layer * 640 : layer * 640 + 640].reshape(blocks, rows, 640)[:, own_rows, :]
        return tuple(
            lines[:, at : at + rows].reshape(WIDE).astype(F32)[None, :] for at in (0, 128)
        )

    use_kernels = span % 128 == 0
    if use_kernels:
        attend_call = functools.partial(attend, ids)
        attend_back_call = functools.partial(attend_back, ids)
    else:
        attend_call = functools.partial(plain_attend, places)
        attend_back_call = functools.partial(plain_attend_back, places)

    columns = w_gate.shape[2]
    shares = [attn_share(layer) for layer in range(DECODER_LAYERS)]
    front_w = gather(jnp.concatenate([*shares, mlp_share(0)], axis=1))
    mlp_w = [(front_w, DECODER_LAYERS)]
    for layer in range(1, DECODER_LAYERS):
        mlp_w.append((gather(mlp_share(layer)), 0))

    hidden = mm(tokens[0], spread)
    kept = []
    for layer in range(DECODER_LAYERS):
        weights = front_w
        gain_a, gain_m = gains_of(weights, layer)
        attn_in, query, pair, _ = project(hidden, gain_a, weights, layer, cosine, sine, model_width)
        around = [pair]
        for shift in range(1, n_ctx):
            around.append(
                lax.ppermute(pair, "ctx", [(i, (i + shift) % n_ctx) for i in range(n_ctx)])
            )
        pairs = jnp.concatenate(around, axis=1)
        mixed, total, _ = attend_call(query, pairs)
        first, last, mid, mlp_in, _ = out_forward(mixed, weights, layer, hidden, gain_m, model_width)
        result, gate, up, _ = mlp_forward(mlp_in, mid, *mlp_w[layer], columns)
        kept.append(
            (hidden, weights, gain_a, gain_m, attn_in, query, pairs, mixed, total, first, last, mid, mlp_in, gate, up)
        )
        hidden = result
    block_out = mm(hidden.astype(BF), spread, NT).astype(BF)[None]

    core = tp_rank % 2
    grad_run = mm(out_grad[0], spread)
    grad_in = grad_run.astype(BF)
    blank = jnp.zeros_like(grad_run)
    mlp_done, attn_done = [None] * DECODER_LAYERS, [None] * DECODER_LAYERS
    for layer in reversed(range(DECODER_LAYERS)):
        (hidden, weights, gain_a, gain_m, attn_in, query, pairs, mixed, total, first, last, mid, mlp_in, gate, up) = kept[layer]
        sources = (gate, up, *mlp_w[layer])
        final = layer == 0
        ready = ()
        if final:
            ready = tips(attn_sum.advance()[:2])
        order = jnp.arange(4, dtype=jnp.int32)
        back, parts, token = mlp_backward(order, 1, grad_in, mlp_in, blank, *sources)
        mlp_done[layer] = lax.psum_scatter(
            parts.reshape(4 * WIDE, -1), ("tp", "shard", "ctx"), scatter_dimension=0, tiled=True
        )
        mid_g, rounded, mixed_g, gain_m_grad, _ = out_backward(
            back, mid, grad_run, gain_m, weights, layer, model_width, after=ready
        )
        ready = ()
        if final:
            ready = tips(attn_sum.advance(token[0]))
        query_g, pair_g, token = attend_back_call(query, pairs, mixed_g, mixed, total, cosine_t, sine_t)
        if final:
            attn_sum.advance(token[0])
            ready = ready + tips(mlp_done[layer + 1 :])
        arrived = [
            lax.ppermute(
                pair_g[:, shift * local_length : (shift + 1) * local_length].astype(BF),
                "ctx",
                [(i, (i - shift) % n_ctx) for i in range(n_ctx)],
            )
            for shift in range(1, n_ctx)
        ]
        back, early, mixed_w, token = query_backward(
            query_g, attn_in, rounded, first, last, weights, layer, after=ready
        )
        grad_run, grad_in, late, gain_a_grad, token = key_backward(
            pair_g,
            arrived,
            query_g,
            back,
            mixed_w,
            attn_in,
            weights,
            layer,
            hidden,
            mid_g,
            gain_a,
            cosine,
            sine,
            model_width,
        )
        if final:
            attn_done[layer + 1] = attn_sum.advance(token[0])[0]
        lines = jnp.concatenate(
            [
                jnp.pad(gain_a_grad.reshape(blocks, rows), ((0, 0), (0, 128 - rows))),
                jnp.pad(gain_m_grad.reshape(blocks, rows), ((0, 0), (0, 640 - 128 - rows))),
            ],
            axis=1,
        ).astype(BF)
        at = lax.broadcasted_iota(jnp.int32, (1, rows, 1), 1)
        second_w = jnp.where(at == own_rows, lines[:, None, :], late[0].reshape(blocks, rows, 640))
        second_w = second_w.reshape(WIDE, 640)
        there, here = [], []
        for part in (slice(0, WIDE // 2), slice(WIDE // 2, WIDE)):
            parts = early[0, part], second_w[part], late[1, part], early[1, part]
            there.append(
                jnp.stack([jnp.where(core == 0, parts[1], parts[0]), jnp.where(core == 0, parts[3], parts[2])])
            )
            here.append(
                jnp.stack([jnp.where(core == 0, parts[0], parts[1]), jnp.where(core == 0, parts[2], parts[3])])
            )
        attn_sum = Reduction(there, here, n_shard, n_ctx, rows)
    for _ in range(4):
        attn_sum.advance()
    attn_done[0] = attn_sum.values[0]
    attn_done = gather_core(gather_pair(jnp.stack(attn_done)), 1)

    grad_high = grad_run.astype(BF)
    grad_low = (grad_run - grad_high.astype(F32)).astype(BF)
    tokens_grad = (mm(grad_high, spread, NT) + mm(grad_low, spread, NT))[None]

    outs = [[] for _ in range(9)]
    for layer, mlp in enumerate(mlp_done):
        attn = attn_done[:, :, layer].reshape(4, rows, 640)
        line = attn[1, own_rows].astype(F32)
        attn = attn[:, :own_rows].transpose(1, 0, 2).reshape(own_rows, 2560).astype(F32)
        mlp = mlp[:own_rows].astype(F32)
        columns = mlp.shape[1] // 3
        for slot, value in enumerate(
            (
                attn[:, :960],
                attn[:, 960:1280],
                attn[:, 1280:1600],
                attn[:, 1600:].T,
                line[:own_rows],
                line[128 : 128 + own_rows],
                mlp[:, :columns],
                mlp[:, columns : 2 * columns],
                mlp[:, 2 * columns :].T,
            )
        ):
            outs[slot].append(value)
    return (block_out, tokens_grad, *[jnp.stack(parts) for parts in outs])


def solution(mesh):
    return jax.shard_map(
        local,
        mesh=mesh,
        in_specs=(
            P(("shard", "tp"), "ctx", None),
            P(),
            P(None, ("shard", "ctx"), None),
            P(None, ("shard", "ctx"), None),
            P(None, ("shard", "ctx"), None),
            P(None, None, ("shard", "ctx")),
            P(None, ("shard", "ctx")),
            P(None, ("shard", "ctx")),
            P(None, ("shard", "ctx"), "tp"),
            P(None, ("shard", "ctx"), "tp"),
            P(None, "tp", ("shard", "ctx")),
            P(("shard", "tp"), "ctx", None),
        ),
        out_specs=(
            P(("shard", "tp"), "ctx", None),
            P(("shard", "tp"), "ctx", None),
            P(None, ("shard", "ctx"), None),
            P(None, ("shard", "ctx"), None),
            P(None, ("shard", "ctx"), None),
            P(None, None, ("shard", "ctx")),
            P(None, ("shard", "ctx")),
            P(None, ("shard", "ctx")),
            P(None, ("shard", "ctx"), "tp"),
            P(None, ("shard", "ctx"), "tp"),
            P(None, "tp", ("shard", "ctx")),
        ),
        check_vma=False,
    )
```

```python
import functools

import jax
import jax.numpy as jnp
from jax import lax
from jax.experimental import pallas as pl
from jax.experimental.pallas import tpu as pltpu
from jax.sharding import PartitionSpec as P

QUERY_HEADS = 15
KEY_VALUE_HEADS = 5
GROUP = QUERY_HEADS // KEY_VALUE_HEADS
HEAD_DIM = 64
DECODER_LAYERS = 2
WIDE = 1024

EPS = 1e-05
THETA = 10000.0
MASKED = -1e30
LOG2E = 1.4426950408889634
SCALE = HEAD_DIM**-0.5
BF = jnp.bfloat16
F32 = jnp.float32
VMEM_LIMIT = 60 * 1024 * 1024

NN = (((1,), (0,)), ((), ()))
NT = (((1,), (1,)), ((), ()))
TN = (((0,), (0,)), ((), ()))


def mm(left, right, dims=NN):
    return lax.dot_general(left, right, dims, preferred_element_type=F32)


CORE_SWAP = [(0, 1), (1, 0), (2, 3), (3, 2)]
PAIR_SWAP = [(0, 2), (2, 0), (1, 3), (3, 1)]


def pick(array, index, axis):
    return lax.dynamic_index_in_dim(array, index, axis, keepdims=False)


def pick_sum(arrays, index, axis):
    total = pick(arrays[0], index, axis)
    for array in arrays[1:]:
        total = total + pick(array, index, axis)
    return total


def tips(arrays):
    return tuple(array[(0,) * (array.ndim - 2)][:8, :128] for array in arrays)


def line_reduce(arrays, axis, name, start=0):
    count = arrays[0].shape[axis]
    rank = lax.axis_index(name)
    total = pick_sum(arrays, rank, axis).astype(F32)
    for shift in range(1, count):
        sent = pick_sum(arrays, (rank + shift) % count + start, axis)
        total += lax.ppermute(
            sent, name, [(i, (i + shift) % count) for i in range(count)]
        ).astype(F32)
    return total.astype(BF)


def pair_reduce(arrays, axis, start=0):
    pair = lax.axis_index("tp") // 2
    sent = lax.ppermute(pick_sum(arrays, 1 - pair + start, axis), "tp", PAIR_SWAP)
    return pick_sum(arrays, pair, axis) + sent


class Reduction:
    def __init__(self, there, here, n_shard, n_ctx, rows):
        self.shape = (2, n_shard // 2, n_ctx, rows, there[0].shape[-1])
        self.stage = 0
        self.values = (there, here)

    def advance(self, start=0):
        self.stage += 1
        if self.stage == 1:
            there, here = self.values
            came = tuple(lax.ppermute(part, "tp", CORE_SWAP) for part in there)
            self.values = came + tuple(here)
        elif self.stage == 2:
            parts = [part.reshape(self.shape) for part in self.values]
            self.values = (
                pair_reduce(parts[0::2], 0, start),
                line_reduce(parts[1::2], 2, "ctx", start),
            )
        elif self.stage == 3:
            first, second = self.values
            self.values = (
                line_reduce([first], 1, "ctx", start),
                pair_reduce([second], 0, start),
            )
        elif self.stage == 4:
            joined = jnp.concatenate(self.values, axis=0)
            self.values = (line_reduce([joined], 0, "shard", start),)
        return self.values


def gather_pair(array):
    pair = lax.axis_index("tp") // 2
    far = lax.ppermute(array, "tp", PAIR_SWAP)
    return jnp.stack([jnp.where(pair == 0, array, far), jnp.where(pair == 0, far, array)])


def gather_core(array, axis):
    core = lax.axis_index("tp") % 2
    far = lax.ppermute(array, "tp", CORE_SWAP)
    return jnp.stack([jnp.where(core == 0, array, far), jnp.where(core == 0, far, array)], axis=axis)


def call(kernel, grid, in_specs, out_specs, out_shape, scratch, flops, moved, operands, after=(), scalars=()):
    used = len(scalars) + len(operands)
    outs = len(out_shape)

    def body(*refs):
        kept = refs[used + len(after) :]
        kept[outs][0] = 0
        kernel(*refs[:used], *kept[:outs], *kept[outs + 1 :])

    return pl.pallas_call(
        body,
        grid_spec=pltpu.PrefetchScalarGridSpec(
            num_scalar_prefetch=len(scalars),
            grid=grid,
            in_specs=list(in_specs) + [pl.BlockSpec(memory_space=pl.ANY)] * len(after),
            out_specs=list(out_specs) + [pl.BlockSpec(memory_space=pltpu.SMEM)],
            scratch_shapes=scratch,
        ),
        out_shape=list(out_shape) + [jax.ShapeDtypeStruct((1,), jnp.int32)],
        compiler_params=pltpu.CompilerParams(vmem_limit_bytes=VMEM_LIMIT),
        cost_estimate=pl.CostEstimate(flops=flops, bytes_accessed=moved, transcendentals=0),
    )(*scalars, *operands, *after)


def full(*shape):
    return pl.BlockSpec(shape, lambda *at: (0,) * len(shape))


def row_steps(rows):
    step = 256 if rows % 256 == 0 else rows
    return [pl.ds(at, step) for at in range(0, rows, step)]


def mlp_forward_kernel(normed_ref, mid_ref, gate_w, up_w, down_w, out_ref, gate_ref, up_ref):
    @pl.when(pl.program_id(0) == 0)
    def _():
        out_ref[...] = mid_ref[...]

    for part in row_steps(normed_ref.shape[0]):
        normed = normed_ref[part, :]
        gate = mm(normed, gate_w[0])
        up = mm(normed, up_w[0])
        gate_ref[0, part, :] = gate
        up_ref[0, part, :] = up
        inner = (gate * jax.nn.sigmoid(gate) * up).astype(BF)
        out_ref[part, :] += mm(inner, down_w[0], NT)


def mlp_forward(normed, mid, weights, start, columns, after=()):
    rows = normed.shape[0]
    parts = weights.shape[0]
    whole = full(rows, WIDE)
    kept = pl.BlockSpec((1, rows, columns), lambda t: (t, 0, 0))
    return call(
        mlp_forward_kernel,
        (parts,),
        [whole, whole]
        + [
            pl.BlockSpec((1, WIDE, columns), functools.partial(lambda c, t: (t, 0, c), start + c))
            for c in range(3)
        ],
        [whole, kept, kept],
        [
            jax.ShapeDtypeStruct((rows, WIDE), F32),
            jax.ShapeDtypeStruct((parts, rows, columns), F32),
            jax.ShapeDtypeStruct((parts, rows, columns), F32),
        ],
        [],
        6 * rows * WIDE * columns * parts,
        WIDE * columns * parts * 6 + rows * (WIDE * 10 + columns * parts * 8),
        (normed, mid, weights, weights, weights),
        after,
    )


def mlp_backward_kernel(
    order_ref,
    grad_ref,
    normed_ref,
    base_ref,
    gate_ref,
    up_ref,
    gate_w,
    up_w,
    down_w,
    back_ref,
    *rest,
):
    *outs, inner, gate_g, up_g = rest
    @pl.when(pl.program_id(0) == 0)
    def _():
        back_ref[...] = base_ref[...]

    columns = gate_ref.shape[2]
    for part in row_steps(grad_ref.shape[0]):
        act_grad = mm(grad_ref[part, :], down_w[0])
        gate = gate_ref[0, part, :]
        up = up_ref[0, part, :]
        sig = jax.nn.sigmoid(gate)
        silu = gate * sig
        inner[part, :] = (silu * up).astype(BF)
        gate_part = (act_grad * up * sig * (1.0 + gate * (1.0 - sig))).astype(BF)
        up_part = (act_grad * silu).astype(BF)
        gate_g[part, :] = gate_part
        up_g[part, :] = up_part
        back_ref[part, :] += mm(gate_part, gate_w[0], NT) + mm(up_part, up_w[0], NT)
    for at in range(0, WIDE, 256):
        part = pl.ds(at, 256)
        normed = normed_ref[:, part]
        out_w = outs[at * len(outs) // WIDE]
        part = pl.ds(at % (WIDE // len(outs)), 256)
        out_w[0, part, 0:columns] = mm(normed, gate_g[...], TN).astype(BF)
        out_w[0, part, columns : 2 * columns] = mm(normed, up_g[...], TN).astype(BF)
        out_w[0, part, 2 * columns : 3 * columns] = mm(grad_ref[:, pl.ds(at, 256)], inner[...], TN).astype(BF)


def mlp_backward(order, pieces, grad, normed, base, gate, up, weights, start, after=()):
    rows, columns = gate.shape[1:]
    parts = order.shape[0]
    whole = full(rows, WIDE)
    kept = pl.BlockSpec((1, rows, columns), lambda i, order: (order[i], 0, 0))
    weight_parts = [
        pl.BlockSpec((1, WIDE, columns), functools.partial(lambda c, i, order: (order[i], 0, c), start + c))
        for c in range(3)
    ]
    return call(
        mlp_backward_kernel,
        (parts,),
        [whole, whole, whole, kept, kept] + weight_parts,
        [whole] + [pl.BlockSpec((1, WIDE // pieces, 3 * columns), lambda i, order: (i, 0, 0))] * pieces,
        [jax.ShapeDtypeStruct((rows, WIDE), F32)]
        + [jax.ShapeDtypeStruct((parts, WIDE // pieces, 3 * columns), BF)] * pieces,
        [pltpu.VMEM((rows, columns), BF)] * 3,
        12 * rows * WIDE * columns * parts,
        parts * WIDE * columns * 12 + rows * (WIDE * 12 + columns * parts * 8),
        (grad, normed, base, gate, up, weights, weights, weights),
        after,
        (order,),
    )


def turn_pairs(values):
    lane = lax.broadcasted_iota(jnp.int32, values.shape, 1) % HEAD_DIM
    return jnp.where(
        lane < HEAD_DIM // 2, -pltpu.roll(values, 96, 1), pltpu.roll(values, 32, 1)
    )


def low_lanes(values):
    lane = lax.broadcasted_iota(jnp.int32, values.shape, 1)
    return jnp.where(lane < HEAD_DIM, values, jnp.zeros_like(values))


def high_lanes(values):
    lane = lax.broadcasted_iota(jnp.int32, values.shape, 1)
    return jnp.where(lane < HEAD_DIM, jnp.zeros_like(values), values)


def other_half(values):
    return jnp.concatenate([values[:, HEAD_DIM:], values[:, :HEAD_DIM]], axis=1)


def row_scale(hidden, width):
    return lax.rsqrt(jnp.sum(hidden * hidden, axis=-1, keepdims=True) / width + EPS)


def project_kernel(width, hidden_ref, gain_ref, weights_ref, cos_ref, sin_ref, normed_ref, query_ref, pair_ref):
    for rows in row_steps(hidden_ref.shape[0]):
        hidden = hidden_ref[rows, :]
        normed = (hidden * row_scale(hidden, width) * gain_ref[...]).astype(BF)
        normed_ref[rows, :] = normed
        cosine, sine = cos_ref[rows, :], sin_ref[rows, :]
        keys = []
        for part in range(3):
            block = mm(normed, weights_ref[part] if part < 2 else weights_ref[part, :, :384])
            for at in range(5 if part < 2 else 3):
                two = block[:, at * 128 : at * 128 + 128]
                if part < 2:
                    two = two * cosine + turn_pairs(two) * sine
                two = two.astype(BF)
                for side in range(2):
                    head = part * 10 + at * 2 + side
                    if head < QUERY_HEADS:
                        query_ref[head, rows, :] = low_lanes(other_half(two) if side else two)
                    elif head < QUERY_HEADS + KEY_VALUE_HEADS:
                        keys.append(low_lanes(other_half(two) if side else two))
                    elif head < QUERY_HEADS + 2 * KEY_VALUE_HEADS:
                        group = head - QUERY_HEADS - KEY_VALUE_HEADS
                        pair_ref[group, rows, :] = keys[group] + high_lanes(two if side else other_half(two))


def project(hidden, gain, weights, layer, cosine, sine, width, after=()):
    rows = hidden.shape[0]
    return call(
        functools.partial(project_kernel, width),
        (1,),
        [
            full(rows, WIDE),
            full(1, WIDE),
            pl.BlockSpec((3, WIDE, 640), lambda i: (0, 0, layer)),
            full(rows, 128),
            full(rows, 128),
        ],
        [full(rows, WIDE), full(QUERY_HEADS, rows, 128), full(KEY_VALUE_HEADS, rows, 128)],
        [
            jax.ShapeDtypeStruct((rows, WIDE), BF),
            jax.ShapeDtypeStruct((QUERY_HEADS, rows, 128), BF),
            jax.ShapeDtypeStruct((KEY_VALUE_HEADS, rows, 128), BF),
        ],
        [],
        2 * rows * WIDE * 1600,
        WIDE * 1600 * 2 + rows * WIDE * 6 + rows * 128 * 48,
        (hidden, gain, weights, cosine, sine),
        after,
    )


def join_heads(heads):
    columns = [heads[0]]
    for at in range(1, len(heads), 2):
        columns.append(other_half(heads[at]) + heads[at + 1])
    return columns


def out_forward_kernel(width, mixed_ref, weights_ref, hidden_ref, gain_ref, first_ref, last_ref, mid_ref, normed_ref):
    for rows in row_steps(hidden_ref.shape[0]):
        heads = [mixed_ref[head, rows, :] for head in range(QUERY_HEADS)]
        blank = jnp.zeros_like(heads[0])
        first = jnp.concatenate([blank, blank] + join_heads(heads[:5]), axis=1)
        pairs = [other_half(heads[at]) + heads[at + 1] for at in range(5, QUERY_HEADS, 2)]
        last = jnp.concatenate(pairs, axis=1)
        first_ref[rows, :] = first
        last_ref[rows, :] = last
        mid = hidden_ref[rows, :] + mm(first, weights_ref[0], NT) + mm(last, weights_ref[1], NT)
        mid_ref[rows, :] = mid
        normed_ref[rows, :] = (mid * row_scale(mid, width) * gain_ref[...]).astype(BF)


def out_forward(mixed, weights, layer, hidden, gain, width, after=()):
    rows = hidden.shape[0]
    return call(
        functools.partial(out_forward_kernel, width),
        (1,),
        [
            full(QUERY_HEADS, rows, 128),
            pl.BlockSpec((2, WIDE, 640), lambda i: (1, 0, layer)),
            full(rows, WIDE),
            full(1, WIDE),
        ],
        [full(rows, 640), full(rows, 640), full(rows, WIDE), full(rows, WIDE)],
        [
            jax.ShapeDtypeStruct((rows, 640), BF),
            jax.ShapeDtypeStruct((rows, 640), BF),
            jax.ShapeDtypeStruct((rows, WIDE), F32),
            jax.ShapeDtypeStruct((rows, WIDE), BF),
        ],
        [],
        4 * rows * WIDE * 640,
        WIDE * 640 * 4 + rows * WIDE * 10 + rows * 6400,
        (mixed, weights, hidden, gain),
        after,
    )


def norm_back(gradient, hidden, gain, width):
    scaling = row_scale(hidden, width)
    normed = hidden * scaling
    weighted = gradient * gain
    inner = jnp.sum(weighted * normed, axis=-1, keepdims=True) / width
    gain_grad = jnp.sum(gradient * normed, axis=0, keepdims=True)
    return scaling * (weighted - normed * inner), gain_grad


def out_backward_kernel(
    width, back_ref, mid_ref, grad_ref, gain_ref, weights_ref, mid_g, rounded_ref, mixed_g, gain_g
):
    gain_g[...] = jnp.zeros_like(gain_g)
    for rows in row_steps(mid_ref.shape[0]):
        change, gain_part = norm_back(back_ref[rows, :], mid_ref[rows, :], gain_ref[...], width)
        gain_g[...] += gain_part
        change += grad_ref[rows, :]
        mid_g[rows, :] = change
        rounded = change.astype(BF)
        rounded_ref[rows, :] = rounded
        for part in range(2):
            block = mm(rounded, weights_ref[part]).astype(BF)
            for at in range(5):
                for side in range(2):
                    head = part * 10 + at * 2 + side - 5
                    if head >= 0:
                        two = block[:, at * 128 : at * 128 + 128]
                        mixed_g[head, rows, :] = high_lanes(two if side else other_half(two))


def out_backward(back, mid, grad, gain, weights, layer, width, after=()):
    rows = mid.shape[0]
    return call(
        functools.partial(out_backward_kernel, width),
        (1,),
        [
            full(rows, WIDE),
            full(rows, WIDE),
            full(rows, WIDE),
            full(1, WIDE),
            pl.BlockSpec((2, WIDE, 640), lambda i: (1, 0, layer)),
        ],
        [full(rows, WIDE), full(rows, WIDE), full(QUERY_HEADS, rows, 128), full(1, WIDE)],
        [
            jax.ShapeDtypeStruct((rows, WIDE), F32),
            jax.ShapeDtypeStruct((rows, WIDE), BF),
            jax.ShapeDtypeStruct((QUERY_HEADS, rows, 128), BF),
            jax.ShapeDtypeStruct((1, WIDE), F32),
        ],
        [],
        4 * rows * WIDE * 640,
        WIDE * 640 * 4 + rows * WIDE * 18 + rows * 3840,
        (back, mid, grad, gain, weights),
        after,
    )


def query_backward_kernel(
    query_g, normed_ref, rounded_ref, mixed_ref, last_ref, weights_ref, back_ref, out_w, mixed_w, first
):
    for rows in row_steps(normed_ref.shape[0]):
        part = jnp.concatenate(
            [query_g[at, rows, :] + other_half(query_g[at + 1, rows, :]) for at in range(0, 10, 2)], axis=1
        )
        first[rows, :] = part
        back_ref[rows, :] = mm(part, weights_ref[0], NT)
    for at in range(0, WIDE, 256):
        part = pl.ds(at, 256)
        out_w[0, part, :] = mm(normed_ref[:, part], first[...], TN).astype(BF)
        rounded = rounded_ref[:, part]
        out_w[1, part, :] = mm(rounded, last_ref[...], TN).astype(BF)
        mixed_w[part, :] = mm(rounded, mixed_ref[...], TN)


def query_backward(query_g, normed, rounded, mixed, last, weights, layer, after=()):
    rows = normed.shape[0]
    return call(
        query_backward_kernel,
        (1,),
        [
            full(10, rows, 128),
            full(rows, WIDE),
            full(rows, WIDE),
            full(rows, 640),
            full(rows, 640),
            pl.BlockSpec((1, WIDE, 640), lambda i: (0, 0, layer)),
        ],
        [full(rows, WIDE), full(2, WIDE, 640), full(WIDE, 640)],
        [
            jax.ShapeDtypeStruct((rows, WIDE), F32),
            jax.ShapeDtypeStruct((2, WIDE, 640), BF),
            jax.ShapeDtypeStruct((WIDE, 640), F32),
        ],
        [pltpu.VMEM((rows, 640), BF)],
        8 * rows * WIDE * 640,
        WIDE * 640 * 10 + rows * WIDE * 8 + rows * 5120,
        (query_g, normed, rounded, mixed, last, weights),
        after,
    )


def key_backward_kernel(width, shares, *refs):
    pairs = refs[:shares]
    query_g, back_ref, mixed_w, normed_ref, weights_ref, hidden_ref, mid_g, gain_ref = refs[shares : shares + 8]
    cos_ref, sin_ref, grad_ref, rounded_ref, out_w, gain_g, second, third = refs[shares + 8 :]
    gain_g[...] = jnp.zeros_like(gain_g)
    for rows in row_steps(hidden_ref.shape[0]):
        keys, values = [], []
        for group in range(KEY_VALUE_HEADS):
            pair = pairs[0][group, rows, :]
            for other in pairs[1:]:
                pair = pair + other[group, rows, :].astype(F32)
            moved = pair * sin_ref[rows, :]
            lane = lax.broadcasted_iota(jnp.int32, pair.shape, 1)
            turned = jnp.where(lane < HEAD_DIM // 2, pltpu.roll(moved, 96, 1), -pltpu.roll(moved, 32, 1))
            key = pair * cos_ref[rows, :] + turned
            keys.append(low_lanes(key).astype(BF))
            values.append(high_lanes(pair).astype(BF))
        heads = [query_g[at, rows, :] for at in range(5)] + keys
        second_part = jnp.concatenate(
            [heads[at] + other_half(heads[at + 1]) for at in range(0, 10, 2)], axis=1
        )
        third_part = jnp.concatenate(
            [other_half(values[0]) + values[1], other_half(values[2]) + values[3], other_half(values[4])],
            axis=1,
        )
        second[rows, :] = second_part
        third[rows, :] = third_part
        back = (
            back_ref[rows, :]
            + mm(second_part, weights_ref[1], NT)
            + mm(third_part, weights_ref[2, :, :384], NT)
        )
        change, gain_part = norm_back(back, hidden_ref[rows, :], gain_ref[...], width)
        gain_g[...] += gain_part
        grad = mid_g[rows, :] + change
        grad_ref[rows, :] = grad
        rounded_ref[rows, :] = grad.astype(BF)
    for at in range(0, WIDE, 256):
        part = pl.ds(at, 256)
        normed = normed_ref[:, part]
        out_w[0, part, :] = mm(normed, second[...], TN).astype(BF)
        out_w[1, part, :384] = (mm(normed, third[...], TN) + mixed_w[part, :384]).astype(BF)
        out_w[1, part, 384:] = mixed_w[part, 384:].astype(BF)


def key_backward(
    pair_g, arrived, query_g, back, mixed_w, normed, weights, layer, hidden, mid_g, gain, cosine, sine, width, after=()
):
    rows = hidden.shape[0]
    own = pl.BlockSpec((KEY_VALUE_HEADS, rows, 128), lambda i: (0, 0, 0))
    return call(
        functools.partial(key_backward_kernel, width, 1 + len(arrived)),
        (1,),
        [own] * (1 + len(arrived))
        + [
            pl.BlockSpec((5, rows, 128), lambda i: (2, 0, 0)),
            full(rows, WIDE),
            full(WIDE, 640),
            full(rows, WIDE),
            pl.BlockSpec((3, WIDE, 640), lambda i: (0, 0, layer)),
            full(rows, WIDE),
            full(rows, WIDE),
            full(1, WIDE),
            full(rows, 128),
            full(rows, 128),
        ],
        [full(rows, WIDE), full(rows, WIDE), full(2, WIDE, 640), full(1, WIDE)],
        [
            jax.ShapeDtypeStruct((rows, WIDE), F32),
            jax.ShapeDtypeStruct((rows, WIDE), BF),
            jax.ShapeDtypeStruct((2, WIDE, 640), BF),
            jax.ShapeDtypeStruct((1, WIDE), F32),
        ],
        [pltpu.VMEM((rows, 640), BF), pltpu.VMEM((rows, 384), BF)],
        7 * rows * WIDE * 640,
        WIDE * 640 * 12 + rows * WIDE * 20 + rows * 12800,
        (pair_g, *arrived, query_g, back, mixed_w, normed, weights, hidden, mid_g, gain, cosine, sine),
        after,
    )


def diagonal_bias(span):
    key_at = lax.broadcasted_iota(jnp.int32, (span, span), 0)
    query_at = lax.broadcasted_iota(jnp.int32, (span, span), 1)
    return jnp.concatenate([jnp.where(key_at <= query_at, 0.0, MASKED)] * GROUP, axis=1)


def turn_rows(pair_ref, turned, lanes):
    span = pair_ref.shape[1] // 2
    for at in range(0, pair_ref.shape[1], span):
        turned[:, at : at + span] = pair_ref[0, at : at + span, :].astype(F32).T[lanes, :].astype(BF)


def attend_more(query, pair_ref, turned, at, top, norm, mixed):
    more = mm(pair_ref[0, at, :], query, NT) * (SCALE * LOG2E)
    old = top[...]
    peak = jnp.maximum(old, jnp.max(more, axis=0, keepdims=True))
    keep = jnp.exp2(old - peak)
    weight = jnp.exp2(more - peak)
    top[...] = peak
    norm[...] = norm[...] * keep + jnp.sum(weight, axis=0, keepdims=True)
    mixed[...] = mixed[...] * keep + mm(turned[:, at], weight.astype(BF))


def attend_own_kernel(ids_ref, query_ref, pair_ref, top_ref, norm_ref, mixed_ref, turned):
    span = query_ref.shape[1] // 2
    width = GROUP * span
    turn_rows(pair_ref, turned, slice(HEAD_DIM, 2 * HEAD_DIM))
    bias = diagonal_bias(span)
    for s in range(2):
        own, other = slice(s * span, (s + 1) * span), slice((1 - s) * span, (2 - s) * span)
        query = query_ref[:, own, :].reshape(width, 128)
        first = mm(pair_ref[0, own, :], query, NT) * (SCALE * LOG2E) + bias
        peak = jnp.max(first, axis=0, keepdims=True)
        weight = jnp.exp2(first - peak)
        top_ref[0, s] = peak
        norm_ref[0, s] = jnp.sum(weight, axis=0, keepdims=True)
        mixed_ref[0, s] = mm(turned[:, own], weight.astype(BF))

        @pl.when(ids_ref[1 - s] < ids_ref[s])
        def _():
            attend_more(query, pair_ref, turned, other, top_ref.at[0, s], norm_ref.at[0, s], mixed_ref.at[0, s])


def attend_far_kernel(
    ids_ref, query_ref, pair_ref, top_ref, norm_ref, mixed_ref, out_ref, total_ref, turned, top, norm, mixed
):
    span = query_ref.shape[1] // 2
    width = GROUP * span
    turn_rows(pair_ref, turned, slice(HEAD_DIM, 2 * HEAD_DIM))
    for s in range(2):
        own = slice(s * span, (s + 1) * span)
        query = query_ref[:, own, :].reshape(width, 128)
        top[...] = top_ref[0, s]
        norm[...] = norm_ref[0, s]
        mixed[...] = mixed_ref[0, s]
        for j in range(pair_ref.shape[1] // span):

            @pl.when(ids_ref[2 + j] < ids_ref[s])
            def _():
                attend_more(query, pair_ref, turned, slice(j * span, (j + 1) * span), top, norm, mixed)

        total_ref[0, s] = top[...] + jnp.log2(norm[...])
        result = mixed[...] / norm[...]
        result = jnp.concatenate([jnp.zeros_like(result), result], axis=0).T.astype(BF)
        out_ref[:, own, :] = result.reshape(GROUP, span, 128)


def group_specs(rows, keys):
    width = GROUP * rows // 2
    return (
        pl.BlockSpec((GROUP, rows, 128), lambda g, ids: (g, 0, 0)),
        pl.BlockSpec((1, keys, 128), lambda g, ids: (g, 0, 0)),
        pl.BlockSpec((1, 2, 1, width), lambda g, ids: (g, 0, 0, 0)),
        pl.BlockSpec((1, 2, HEAD_DIM, width), lambda g, ids: (g, 0, 0, 0)),
    )


def attend(ids, query, pair, far):
    rows = query.shape[1]
    keys = far.shape[1]
    width = GROUP * rows // 2
    line = jax.ShapeDtypeStruct((KEY_VALUE_HEADS, 2, 1, width), F32)
    block = jax.ShapeDtypeStruct((KEY_VALUE_HEADS, 2, HEAD_DIM, width), F32)
    heads, near, lines, blocks = group_specs(rows, rows)
    *state, _ = call(
        attend_own_kernel,
        (KEY_VALUE_HEADS,),
        [heads, near],
        [lines, lines, blocks],
        [line, line, block],
        [pltpu.VMEM((HEAD_DIM, rows), BF)],
        8 * QUERY_HEADS * rows * rows * 128,
        QUERY_HEADS * rows * 1024,
        (query, pair),
        (),
        (ids,),
    )
    heads, there, lines, blocks = group_specs(rows, keys)
    return call(
        attend_far_kernel,
        (KEY_VALUE_HEADS,),
        [heads, there, lines, lines, blocks],
        [heads, lines],
        [jax.ShapeDtypeStruct((QUERY_HEADS, rows, 128), BF), line],
        [
            pltpu.VMEM((HEAD_DIM, keys), BF),
            pltpu.VMEM((1, width), F32),
            pltpu.VMEM((1, width), F32),
            pltpu.VMEM((HEAD_DIM, width), F32),
        ],
        8 * QUERY_HEADS * rows * keys * 128,
        QUERY_HEADS * rows * 1536,
        (query, far, *state),
        (),
        (ids,),
    )


def attend_back_block(pair_ref, at, query, grad, total, deltas, turned, bias, pair_g):
    pair = pair_ref[0, at, :]
    scores = mm(pair, query, NT) * (SCALE * LOG2E) - total
    if bias is not None:
        scores = scores + bias
    weight = jnp.exp2(scores)
    change = (weight * (mm(pair, grad, NT) - deltas[...])).astype(BF)
    pair_g[at, :] += mm(change, query) * SCALE + mm(weight.astype(BF), grad)
    return mm(turned[:, at], change)


def row_products(grad_ref, out_ref, own, width):
    product = grad_ref[:, own, :].astype(F32) * out_ref[:, own, :].astype(F32)
    return jnp.sum(product.reshape(width, 128).T, axis=0, keepdims=True)


def attend_back_far_kernel(
    ids_ref, query_ref, pair_ref, grad_ref, out_ref, total_ref, mixed_ref, pair_out, turned, deltas, pair_g
):
    span = query_ref.shape[1] // 2
    width = GROUP * span
    turn_rows(pair_ref, turned, slice(0, HEAD_DIM))
    pair_g[...] = jnp.zeros_like(pair_g)
    mixed_ref[...] = jnp.zeros_like(mixed_ref)
    for s in range(2):
        own = slice(s * span, (s + 1) * span)
        query = query_ref[:, own, :].reshape(width, 128)
        grad = grad_ref[:, own, :].reshape(width, 128)
        deltas[...] = row_products(grad_ref, out_ref, own, width)
        for j in range(pair_ref.shape[1] // span):

            @pl.when(ids_ref[2 + j] < ids_ref[s])
            def _():
                at = slice(j * span, (j + 1) * span)
                mixed_ref[0, s] += attend_back_block(
                    pair_ref, at, query, grad, total_ref[0, s], deltas, turned, None, pair_g
                )

    pair_out[0] = pair_g[...].astype(BF)


def attend_back_own_kernel(
    ids_ref,
    query_ref,
    pair_ref,
    grad_ref,
    out_ref,
    total_ref,
    mixed_ref,
    cos_ref,
    sin_ref,
    query_g,
    pair_out,
    turned,
    deltas,
    mixed,
    pair_g,
):
    span = query_ref.shape[1] // 2
    width = GROUP * span
    half = HEAD_DIM // 2
    turn_rows(pair_ref, turned, slice(0, HEAD_DIM))
    pair_g[...] = jnp.zeros_like(pair_g)
    bias = diagonal_bias(span)
    for s in range(2):
        own, other = slice(s * span, (s + 1) * span), slice((1 - s) * span, (2 - s) * span)
        query = query_ref[:, own, :].reshape(width, 128)
        grad = grad_ref[:, own, :].reshape(width, 128)
        deltas[...] = row_products(grad_ref, out_ref, own, width)
        total = total_ref[0, s]
        mixed[...] = mixed_ref[0, s] + attend_back_block(
            pair_ref, own, query, grad, total, deltas, turned, bias, pair_g
        )

        @pl.when(ids_ref[1 - s] < ids_ref[s])
        def _():
            mixed[...] += attend_back_block(
                pair_ref, other, query, grad, total_ref[0, s], deltas, turned, None, pair_g
            )

        cosine = jnp.concatenate([cos_ref[:, own]] * GROUP, axis=1)
        sine = jnp.concatenate([sin_ref[:, own]] * GROUP, axis=1)
        change = mixed[...] * SCALE
        moved = change * sine
        change = change * cosine + jnp.concatenate([moved[half:], -moved[:half]], axis=0)
        change = jnp.concatenate([change, jnp.zeros_like(change)], axis=0).T.astype(BF)
        query_g[:, own, :] = change.reshape(GROUP, span, 128)
    pair_out[0] = pair_g[...]


def attend_back_far(ids, query, far, grad, out, total):
    rows = query.shape[1]
    keys = far.shape[1]
    width = GROUP * rows // 2
    heads, there, lines, blocks = group_specs(rows, keys)
    return call(
        attend_back_far_kernel,
        (KEY_VALUE_HEADS,),
        [heads, there, heads, heads, lines],
        [blocks, there],
        [
            jax.ShapeDtypeStruct((KEY_VALUE_HEADS, 2, HEAD_DIM, width), F32),
            jax.ShapeDtypeStruct((KEY_VALUE_HEADS, keys, 128), BF),
        ],
        [pltpu.VMEM((HEAD_DIM, keys), BF), pltpu.VMEM((1, width), F32), pltpu.VMEM((keys, 128), F32)],
        20 * QUERY_HEADS * rows * keys * 128,
        QUERY_HEADS * rows * 2048,
        (query, far, grad, out, total),
        (),
        (ids,),
    )


def attend_back_own(ids, query, pair, grad, out, total, mixed, cosine_t, sine_t):
    rows = query.shape[1]
    width = GROUP * rows // 2
    heads, near, lines, blocks = group_specs(rows, rows)
    return call(
        attend_back_own_kernel,
        (KEY_VALUE_HEADS,),
        [heads, near, heads, heads, lines, blocks, full(HEAD_DIM, rows), full(HEAD_DIM, rows)],
        [heads, near],
        [
            jax.ShapeDtypeStruct((QUERY_HEADS, rows, 128), BF),
            jax.ShapeDtypeStruct((KEY_VALUE_HEADS, rows, 128), F32),
        ],
        [
            pltpu.VMEM((HEAD_DIM, rows), BF),
            pltpu.VMEM((1, width), F32),
            pltpu.VMEM((HEAD_DIM, width), F32),
            pltpu.VMEM((rows, 128), F32),
        ],
        20 * QUERY_HEADS * rows * rows * 128,
        QUERY_HEADS * rows * 2560,
        (query, pair, grad, out, total, mixed, cosine_t, sine_t),
        (),
        (ids,),
    )


def plain_scores(query, pairs, places, own):
    grouped = query[..., :HEAD_DIM].reshape(KEY_VALUE_HEADS, GROUP, -1, HEAD_DIM)
    scores = jnp.einsum("kgqd,ktd->kgqt", grouped, pairs[..., :HEAD_DIM], preferred_element_type=F32)
    return grouped, jnp.where(places[None, :] <= own[:, None], scores * SCALE, MASKED)


def plain_attend(places, query, pair, far):
    rows = query.shape[1]
    pairs = jnp.concatenate([pair, far], axis=1)
    _, scores = plain_scores(query, pairs, places, places[:rows])
    top = jnp.max(scores, axis=-1, keepdims=True)
    weight = jnp.exp(scores - top)
    norm = jnp.sum(weight, axis=-1, keepdims=True)
    mixed = jnp.einsum(
        "kgqt,ktd->kgqd", (weight / norm).astype(BF), pairs[..., HEAD_DIM:], preferred_element_type=F32
    )
    mixed = jnp.pad(mixed.reshape(QUERY_HEADS, rows, HEAD_DIM), ((0, 0), (0, 0), (HEAD_DIM, 0)))
    return mixed.astype(BF), top + jnp.log(norm), jnp.zeros((1,), jnp.int32)


def plain_attend_back(places, query, pairs, grad, out, total, cosine_t, sine_t, after=()):
    rows = query.shape[1]
    half = HEAD_DIM // 2
    grouped, scores = plain_scores(query, pairs, places, places[:rows])
    weight = jnp.exp(scores - total)
    grad = grad[..., HEAD_DIM:].reshape(grouped.shape)
    reach = jnp.einsum("kgqd,ktd->kgqt", grad, pairs[..., HEAD_DIM:], preferred_element_type=F32)
    change = (weight * (reach - jnp.sum(weight * reach, axis=-1, keepdims=True))).astype(BF)
    query_g = SCALE * jnp.einsum("kgqt,ktd->kgqd", change, pairs[..., :HEAD_DIM], preferred_element_type=F32)
    key_g = SCALE * jnp.einsum("kgqt,kgqd->ktd", change, grouped, preferred_element_type=F32)
    value_g = jnp.einsum("kgqt,kgqd->ktd", weight.astype(BF), grad, preferred_element_type=F32)
    moved = query_g * sine_t.T
    query_g = query_g * cosine_t.T + jnp.concatenate([moved[..., half:], -moved[..., :half]], axis=-1)
    query_g = jnp.pad(query_g.reshape(QUERY_HEADS, rows, HEAD_DIM), ((0, 0), (0, 0), (0, HEAD_DIM)))
    return query_g.astype(BF), jnp.concatenate([key_g, value_g], axis=-1), jnp.zeros((1,), jnp.int32)


def local(
    tokens,
    span_ids,
    w_query,
    key_weight,
    value_weight,
    w_out,
    gain_attn,
    gain_mlp,
    w_gate,
    w_up,
    w_down,
    out_grad,
):
    group_count, local_length, model_width = tokens.shape
    assert group_count == 1
    n_ctx = lax.axis_size("ctx")
    n_shard = lax.axis_size("shard")
    blocks = n_ctx * n_shard
    own_rows = model_width // blocks
    rows = WIDE // blocks
    extra = rows - own_rows
    tp_rank = lax.axis_index("tp")
    ctx_rank = lax.axis_index("ctx")
    span = local_length // 2

    ids = jnp.concatenate(
        [lax.dynamic_slice_in_dim(span_ids, 2 * ((ctx_rank - i) % n_ctx), 2) for i in range(n_ctx)]
    )
    places = (ids[:, None] * span + jnp.arange(span, dtype=jnp.int32)[None, :]).reshape(-1)
    own_place = places[:local_length].astype(F32)
    inverse_freq = THETA ** (-jnp.arange(HEAD_DIM // 2, dtype=F32) * 2.0 / HEAD_DIM)
    angles = own_place[:, None] * jnp.tile(inverse_freq, 4)[None, :]
    cosine, sine = jnp.cos(angles), jnp.sin(angles)
    angles_t = jnp.tile(inverse_freq, 2)[:, None] * own_place[None, :]
    cosine_t, sine_t = jnp.cos(angles_t), jnp.sin(angles_t)

    source = jnp.arange(model_width, dtype=jnp.int32)
    target = source // own_rows * rows + source % own_rows
    spread = (target[:, None] == jnp.arange(WIDE, dtype=jnp.int32)[None, :]).astype(BF)

    def attn_share(layer):
        joined = jnp.concatenate(
            [w_query[layer], key_weight[layer], value_weight[layer], w_out[layer].T], axis=1
        )
        gains = jnp.concatenate(
            [
                jnp.pad(gain_attn[layer], (0, 128 - own_rows)),
                jnp.pad(gain_mlp[layer], (0, 2560 - 128 - own_rows)),
            ]
        )
        joined = jnp.concatenate([joined, gains[None, :], jnp.zeros((extra - 1, 2560), BF)], axis=0)
        return lax.dynamic_slice_in_dim(joined, tp_rank * 640, 640, 1)

    def mlp_share(layer):
        joined = jnp.concatenate([w_gate[layer], w_up[layer], w_down[layer].T], axis=1)
        return jnp.pad(joined, ((0, extra), (0, 0)))

    def gather(share):
        return lax.all_gather(share, ("tp", "shard", "ctx"), axis=0, tiled=True).reshape(
            4, WIDE, share.shape[1]
        )


    def gains_of(weights, layer):
        lines = weights[0, :, layer * 640 : layer * 640 + 640].reshape(blocks, rows, 640)[:, own_rows, :]
        return tuple(
            lines[:, at : at + rows].reshape(WIDE).astype(F32)[None, :] for at in (0, 128)
        )

    use_kernels = span % 128 == 0
    if use_kernels:
        attend_call = functools.partial(attend, ids)
    else:
        attend_call = functools.partial(plain_attend, places)

    columns = w_gate.shape[2]
    shares = [attn_share(layer) for layer in range(DECODER_LAYERS)]
    front_w = gather(jnp.concatenate([*shares, mlp_share(0)], axis=1))
    mlp_w = [(front_w, DECODER_LAYERS)]
    for layer in range(1, DECODER_LAYERS):
        mlp_w.append((gather(mlp_share(layer)), 0))

    hidden = mm(tokens[0], spread)
    kept = []
    for layer in range(DECODER_LAYERS):
        weights = front_w
        gain_a, gain_m = gains_of(weights, layer)
        attn_in, query, pair, _ = project(hidden, gain_a, weights, layer, cosine, sine, model_width)
        far = [
            lax.ppermute(pair, "ctx", [(i, (i + shift) % n_ctx) for i in range(n_ctx)])
            for shift in range(1, n_ctx)
        ]
        far = far[0] if n_ctx == 2 else jnp.concatenate(far, axis=1)
        mixed, total, _ = attend_call(query, pair, far)
        first, last, mid, mlp_in, _ = out_forward(mixed, weights, layer, hidden, gain_m, model_width)
        result, gate, up, _ = mlp_forward(mlp_in, mid, *mlp_w[layer], columns)
        kept.append(
            (hidden, weights, gain_a, gain_m, attn_in, query, pair, far, mixed, total, first, last, mid, mlp_in, gate, up)
        )
        hidden = result
    block_out = mm(hidden.astype(BF), spread, NT).astype(BF)[None]

    core = tp_rank % 2
    grad_run = mm(out_grad[0], spread)
    grad_in = grad_run.astype(BF)
    blank = jnp.zeros_like(grad_run)
    mlp_done, attn_done = [None] * DECODER_LAYERS, [None] * DECODER_LAYERS
    for layer in reversed(range(DECODER_LAYERS)):
        (hidden, weights, gain_a, gain_m, attn_in, query, pair, far, mixed, total, first, last, mid, mlp_in, gate, up) = kept[layer]
        sources = (gate, up, *mlp_w[layer])
        final = layer == 0
        ready = ()
        if final:
            ready = tips(attn_sum.advance()[:2])
        order = jnp.arange(4, dtype=jnp.int32)
        back, parts, token = mlp_backward(order, 1, grad_in, mlp_in, blank, *sources)
        mlp_done[layer] = lax.psum_scatter(
            parts.reshape(4 * WIDE, -1), ("tp", "shard", "ctx"), scatter_dimension=0, tiled=True
        )
        mid_g, rounded, mixed_g, gain_m_grad, _ = out_backward(
            back, mid, grad_run, gain_m, weights, layer, model_width, after=ready
        )
        ready = ()
        if final:
            ready = tips(attn_sum.advance(token[0]))
        if use_kernels:
            part, far_g, _ = attend_back_far(ids, query, far, mixed_g, mixed, total)
        else:
            query_g, pair_g, token = plain_attend_back(
                places, query, jnp.concatenate([pair, far], axis=1), mixed_g, mixed, total, cosine_t, sine_t
            )
            pair_g, far_g = pair_g[:, :local_length], pair_g[:, local_length:].astype(BF)
        arrived = [
            lax.ppermute(
                far_g[:, (shift - 1) * local_length : shift * local_length] if n_ctx > 2 else far_g,
                "ctx",
                [(i, (i - shift) % n_ctx) for i in range(n_ctx)],
            )
            for shift in range(1, n_ctx)
        ]
        if use_kernels:
            query_g, pair_g, token = attend_back_own(
                ids, query, pair, mixed_g, mixed, total, part, cosine_t, sine_t
            )
        if final:
            attn_sum.advance(token[0])
            ready = ready + tips(mlp_done[layer + 1 :])
        back, early, mixed_w, token = query_backward(
            query_g, attn_in, rounded, first, last, weights, layer, after=ready
        )
        grad_run, grad_in, late, gain_a_grad, token = key_backward(
            pair_g,
            arrived,
            query_g,
            back,
            mixed_w,
            attn_in,
            weights,
            layer,
            hidden,
            mid_g,
            gain_a,
            cosine,
            sine,
            model_width,
        )
        if final:
            attn_done[layer + 1] = attn_sum.advance(token[0])[0]
        lines = jnp.concatenate(
            [
                jnp.pad(gain_a_grad.reshape(blocks, rows), ((0, 0), (0, 128 - rows))),
                jnp.pad(gain_m_grad.reshape(blocks, rows), ((0, 0), (0, 640 - 128 - rows))),
            ],
            axis=1,
        ).astype(BF)
        at = lax.broadcasted_iota(jnp.int32, (1, rows, 1), 1)
        second_w = jnp.where(at == own_rows, lines[:, None, :], late[0].reshape(blocks, rows, 640))
        second_w = second_w.reshape(WIDE, 640)
        there, here = [], []
        for part in (slice(0, WIDE // 2), slice(WIDE // 2, WIDE)):
            parts = early[0, part], second_w[part], late[1, part], early[1, part]
            there.append(
                jnp.stack([jnp.where(core == 0, parts[1], parts[0]), jnp.where(core == 0, parts[3], parts[2])])
            )
            here.append(
                jnp.stack([jnp.where(core == 0, parts[0], parts[1]), jnp.where(core == 0, parts[2], parts[3])])
            )
        attn_sum = Reduction(there, here, n_shard, n_ctx, rows)
    for _ in range(4):
        attn_sum.advance()
    attn_done[0] = attn_sum.values[0]
    attn_done = gather_core(gather_pair(jnp.stack(attn_done)), 1)

    grad_high = grad_run.astype(BF)
    grad_low = (grad_run - grad_high.astype(F32)).astype(BF)
    tokens_grad = (mm(grad_high, spread, NT) + mm(grad_low, spread, NT))[None]

    outs = [[] for _ in range(9)]
    for layer, mlp in enumerate(mlp_done):
        attn = attn_done[:, :, layer].reshape(4, rows, 640)
        line = attn[1, own_rows].astype(F32)
        attn = attn[:, :own_rows].transpose(1, 0, 2).reshape(own_rows, 2560).astype(F32)
        mlp = mlp[:own_rows].astype(F32)
        columns = mlp.shape[1] // 3
        for slot, value in enumerate(
            (
                attn[:, :960],
                attn[:, 960:1280],
                attn[:, 1280:1600],
                attn[:, 1600:].T,
                line[:own_rows],
                line[128 : 128 + own_rows],
                mlp[:, :columns],
                mlp[:, columns : 2 * columns],
                mlp[:, 2 * columns :].T,
            )
        ):
            outs[slot].append(value)
    return (block_out, tokens_grad, *[jnp.stack(parts) for parts in outs])


def solution(mesh):
    return jax.shard_map(
        local,
        mesh=mesh,
        in_specs=(
            P(("shard", "tp"), "ctx", None),
            P(),
            P(None, ("shard", "ctx"), None),
            P(None, ("shard", "ctx"), None),
            P(None, ("shard", "ctx"), None),
            P(None, None, ("shard", "ctx")),
            P(None, ("shard", "ctx")),
            P(None, ("shard", "ctx")),
            P(None, ("shard", "ctx"), "tp"),
            P(None, ("shard", "ctx"), "tp"),
            P(None, "tp", ("shard", "ctx")),
            P(("shard", "tp"), "ctx", None),
        ),
        out_specs=(
            P(("shard", "tp"), "ctx", None),
            P(("shard", "tp"), "ctx", None),
            P(None, ("shard", "ctx"), None),
            P(None, ("shard", "ctx"), None),
            P(None, ("shard", "ctx"), None),
            P(None, None, ("shard", "ctx")),
            P(None, ("shard", "ctx")),
            P(None, ("shard", "ctx")),
            P(None, ("shard", "ctx"), "tp"),
            P(None, ("shard", "ctx"), "tp"),
            P(None, "tp", ("shard", "ctx")),
        ),
        check_vma=False,
    )
```

```python
import functools

import jax
import jax.numpy as jnp
from jax import lax
from jax.experimental import pallas as pl
from jax.experimental.pallas import tpu as pltpu
from jax.sharding import PartitionSpec as P

QUERY_HEADS = 15
KEY_VALUE_HEADS = 5
GROUP = QUERY_HEADS // KEY_VALUE_HEADS
HEAD_DIM = 64
DECODER_LAYERS = 2
WIDE = 1024

EPS = 1e-05
THETA = 10000.0
MASKED = -1e30
LOG2E = 1.4426950408889634
SCALE = HEAD_DIM**-0.5
BF = jnp.bfloat16
F32 = jnp.float32
VMEM_LIMIT = 60 * 1024 * 1024

NN = (((1,), (0,)), ((), ()))
NT = (((1,), (1,)), ((), ()))
TN = (((0,), (0,)), ((), ()))


def mm(left, right, dims=NN):
    return lax.dot_general(left, right, dims, preferred_element_type=F32)


CORE_SWAP = [(0, 1), (1, 0), (2, 3), (3, 2)]
PAIR_SWAP = [(0, 2), (2, 0), (1, 3), (3, 1)]


def pick(array, index, axis):
    return lax.dynamic_index_in_dim(array, index, axis, keepdims=False)


def pick_sum(arrays, index, axis):
    total = pick(arrays[0], index, axis)
    for array in arrays[1:]:
        total = total + pick(array, index, axis)
    return total


def tips(arrays):
    return tuple(array[(0,) * (array.ndim - 2)][:8, :128] for array in arrays)


def line_reduce(arrays, axis, name, start=0):
    count = arrays[0].shape[axis]
    rank = lax.axis_index(name)
    total = pick_sum(arrays, rank, axis).astype(F32)
    for shift in range(1, count):
        sent = pick_sum(arrays, (rank + shift) % count + start, axis)
        total += lax.ppermute(
            sent, name, [(i, (i + shift) % count) for i in range(count)]
        ).astype(F32)
    return total.astype(BF)


def pair_reduce(arrays, axis, start=0):
    pair = lax.axis_index("tp") // 2
    sent = lax.ppermute(pick_sum(arrays, 1 - pair + start, axis), "tp", PAIR_SWAP)
    return pick_sum(arrays, pair, axis) + sent


class Reduction:
    def __init__(self, there, here, n_shard, n_ctx, rows):
        self.shape = (2, n_shard // 2, n_ctx, rows, there[0].shape[-1])
        self.stage = 0
        self.values = (there, here)

    def advance(self, start=0):
        self.stage += 1
        if self.stage == 1:
            there, here = self.values
            came = tuple(lax.ppermute(part, "tp", CORE_SWAP) for part in there)
            self.values = came + tuple(here)
        elif self.stage == 2:
            parts = [part.reshape(self.shape) for part in self.values]
            self.values = (
                pair_reduce(parts[0::2], 0, start),
                line_reduce(parts[1::2], 2, "ctx", start),
            )
        elif self.stage == 3:
            first, second = self.values
            self.values = (
                line_reduce([first], 1, "ctx", start),
                pair_reduce([second], 0, start),
            )
        elif self.stage == 4:
            joined = jnp.concatenate(self.values, axis=0)
            self.values = (line_reduce([joined], 0, "shard", start),)
        return self.values


def gather_pair(array):
    pair = lax.axis_index("tp") // 2
    far = lax.ppermute(array, "tp", PAIR_SWAP)
    return jnp.stack([jnp.where(pair == 0, array, far), jnp.where(pair == 0, far, array)])


def gather_core(array, axis):
    core = lax.axis_index("tp") % 2
    far = lax.ppermute(array, "tp", CORE_SWAP)
    return jnp.stack([jnp.where(core == 0, array, far), jnp.where(core == 0, far, array)], axis=axis)


def call(kernel, grid, in_specs, out_specs, out_shape, scratch, flops, moved, operands, after=(), scalars=()):
    used = len(scalars) + len(operands)
    outs = len(out_shape)

    def body(*refs):
        kept = refs[used + len(after) :]
        kept[outs][0] = 0
        kernel(*refs[:used], *kept[:outs], *kept[outs + 1 :])

    return pl.pallas_call(
        body,
        grid_spec=pltpu.PrefetchScalarGridSpec(
            num_scalar_prefetch=len(scalars),
            grid=grid,
            in_specs=list(in_specs) + [pl.BlockSpec(memory_space=pl.ANY)] * len(after),
            out_specs=list(out_specs) + [pl.BlockSpec(memory_space=pltpu.SMEM)],
            scratch_shapes=scratch,
        ),
        out_shape=list(out_shape) + [jax.ShapeDtypeStruct((1,), jnp.int32)],
        compiler_params=pltpu.CompilerParams(vmem_limit_bytes=VMEM_LIMIT),
        cost_estimate=pl.CostEstimate(flops=flops, bytes_accessed=moved, transcendentals=0),
    )(*scalars, *operands, *after)


def full(*shape):
    return pl.BlockSpec(shape, lambda *at: (0,) * len(shape))


def row_steps(rows):
    step = 384 if rows % 384 == 0 else rows
    return [pl.ds(at, step) for at in range(0, rows, step)]


def mlp_forward_kernel(normed_ref, mid_ref, gate_w, up_w, down_w, out_ref, gate_ref, up_ref):
    @pl.when(pl.program_id(0) == 0)
    def _():
        out_ref[...] = mid_ref[...]

    for part in row_steps(normed_ref.shape[0]):
        normed = normed_ref[part, :]
        gate = mm(normed, gate_w[0])
        up = mm(normed, up_w[0])
        gate_ref[0, part, :] = gate
        up_ref[0, part, :] = up
        inner = (gate * jax.nn.sigmoid(gate) * up).astype(BF)
        out_ref[part, :] += mm(inner, down_w[0], NT)


def mlp_forward(normed, mid, weights, start, columns, after=()):
    rows = normed.shape[0]
    parts = weights.shape[0]
    whole = full(rows, WIDE)
    kept = pl.BlockSpec((1, rows, columns), lambda t: (t, 0, 0))
    return call(
        mlp_forward_kernel,
        (parts,),
        [whole, whole]
        + [
            pl.BlockSpec((1, WIDE, columns), functools.partial(lambda c, t: (t, 0, c), start + c))
            for c in range(3)
        ],
        [whole, kept, kept],
        [
            jax.ShapeDtypeStruct((rows, WIDE), F32),
            jax.ShapeDtypeStruct((parts, rows, columns), F32),
            jax.ShapeDtypeStruct((parts, rows, columns), F32),
        ],
        [],
        6 * rows * WIDE * columns * parts,
        WIDE * columns * parts * 6 + rows * (WIDE * 10 + columns * parts * 8),
        (normed, mid, weights, weights, weights),
        after,
    )


def mlp_backward_kernel(
    order_ref,
    grad_ref,
    normed_ref,
    base_ref,
    gate_ref,
    up_ref,
    gate_w,
    up_w,
    down_w,
    back_ref,
    *rest,
):
    *outs, inner, gate_g, up_g = rest
    @pl.when(pl.program_id(0) == 0)
    def _():
        back_ref[...] = base_ref[...]

    columns = gate_ref.shape[2]
    for part in row_steps(grad_ref.shape[0]):
        act_grad = mm(grad_ref[part, :], down_w[0])
        gate = gate_ref[0, part, :]
        up = up_ref[0, part, :]
        sig = jax.nn.sigmoid(gate)
        silu = gate * sig
        inner[part, :] = (silu * up).astype(BF)
        gate_part = (act_grad * up * sig * (1.0 + gate * (1.0 - sig))).astype(BF)
        up_part = (act_grad * silu).astype(BF)
        gate_g[part, :] = gate_part
        up_g[part, :] = up_part
        back_ref[part, :] += mm(gate_part, gate_w[0], NT) + mm(up_part, up_w[0], NT)
    for at in range(0, WIDE, 256):
        part = pl.ds(at, 256)
        normed = normed_ref[:, part]
        out_w = outs[at * len(outs) // WIDE]
        part = pl.ds(at % (WIDE // len(outs)), 256)
        out_w[0, part, 0:columns] = mm(normed, gate_g[...], TN).astype(BF)
        out_w[0, part, columns : 2 * columns] = mm(normed, up_g[...], TN).astype(BF)
        out_w[0, part, 2 * columns : 3 * columns] = mm(grad_ref[:, pl.ds(at, 256)], inner[...], TN).astype(BF)


def mlp_backward(order, pieces, grad, normed, base, gate, up, weights, start, after=()):
    rows, columns = gate.shape[1:]
    parts = order.shape[0]
    whole = full(rows, WIDE)
    kept = pl.BlockSpec((1, rows, columns), lambda i, order: (order[i], 0, 0))
    weight_parts = [
        pl.BlockSpec((1, WIDE, columns), functools.partial(lambda c, i, order: (order[i], 0, c), start + c))
        for c in range(3)
    ]
    return call(
        mlp_backward_kernel,
        (parts,),
        [whole, whole, whole, kept, kept] + weight_parts,
        [whole] + [pl.BlockSpec((1, WIDE // pieces, 3 * columns), lambda i, order: (i, 0, 0))] * pieces,
        [jax.ShapeDtypeStruct((rows, WIDE), F32)]
        + [jax.ShapeDtypeStruct((parts, WIDE // pieces, 3 * columns), BF)] * pieces,
        [pltpu.VMEM((rows, columns), BF)] * 3,
        12 * rows * WIDE * columns * parts,
        parts * WIDE * columns * 12 + rows * (WIDE * 12 + columns * parts * 8),
        (grad, normed, base, gate, up, weights, weights, weights),
        after,
        (order,),
    )


def turn_pairs(values):
    lane = lax.broadcasted_iota(jnp.int32, values.shape, 1) % HEAD_DIM
    return jnp.where(
        lane < HEAD_DIM // 2, -pltpu.roll(values, 96, 1), pltpu.roll(values, 32, 1)
    )


def low_lanes(values):
    lane = lax.broadcasted_iota(jnp.int32, values.shape, 1)
    return jnp.where(lane < HEAD_DIM, values, jnp.zeros_like(values))


def high_lanes(values):
    lane = lax.broadcasted_iota(jnp.int32, values.shape, 1)
    return jnp.where(lane < HEAD_DIM, jnp.zeros_like(values), values)


def other_half(values):
    return jnp.concatenate([values[:, HEAD_DIM:], values[:, :HEAD_DIM]], axis=1)


def row_scale(hidden, width):
    return lax.rsqrt(jnp.sum(hidden * hidden, axis=-1, keepdims=True) / width + EPS)


def project_kernel(width, hidden_ref, gain_ref, weights_ref, cos_ref, sin_ref, normed_ref, query_ref, pair_ref):
    for rows in row_steps(hidden_ref.shape[0]):
        hidden = hidden_ref[rows, :]
        normed = (hidden * row_scale(hidden, width) * gain_ref[...]).astype(BF)
        normed_ref[rows, :] = normed
        cosine, sine = cos_ref[rows, :], sin_ref[rows, :]
        keys = []
        for part in range(3):
            block = mm(normed, weights_ref[part] if part < 2 else weights_ref[part, :, :384])
            for at in range(5 if part < 2 else 3):
                two = block[:, at * 128 : at * 128 + 128]
                if part < 2:
                    two = two * cosine + turn_pairs(two) * sine
                two = two.astype(BF)
                for side in range(2):
                    head = part * 10 + at * 2 + side
                    if head < QUERY_HEADS:
                        query_ref[head, rows, :] = low_lanes(other_half(two) if side else two)
                    elif head < QUERY_HEADS + KEY_VALUE_HEADS:
                        keys.append(low_lanes(other_half(two) if side else two))
                    elif head < QUERY_HEADS + 2 * KEY_VALUE_HEADS:
                        group = head - QUERY_HEADS - KEY_VALUE_HEADS
                        pair_ref[group, rows, :] = keys[group] + high_lanes(two if side else other_half(two))


def project(hidden, gain, weights, layer, cosine, sine, width, after=()):
    rows = hidden.shape[0]
    return call(
        functools.partial(project_kernel, width),
        (1,),
        [
            full(rows, WIDE),
            full(1, WIDE),
            pl.BlockSpec((3, WIDE, 640), lambda i: (0, 0, layer)),
            full(rows, 128),
            full(rows, 128),
        ],
        [full(rows, WIDE), full(QUERY_HEADS, rows, 128), full(KEY_VALUE_HEADS, rows, 128)],
        [
            jax.ShapeDtypeStruct((rows, WIDE), BF),
            jax.ShapeDtypeStruct((QUERY_HEADS, rows, 128), BF),
            jax.ShapeDtypeStruct((KEY_VALUE_HEADS, rows, 128), BF),
        ],
        [],
        2 * rows * WIDE * 1600,
        WIDE * 1600 * 2 + rows * WIDE * 6 + rows * 128 * 48,
        (hidden, gain, weights, cosine, sine),
        after,
    )


def join_heads(heads):
    columns = [heads[0]]
    for at in range(1, len(heads), 2):
        columns.append(other_half(heads[at]) + heads[at + 1])
    return columns


def out_forward_kernel(width, mixed_ref, weights_ref, hidden_ref, gain_ref, first_ref, last_ref, mid_ref, normed_ref):
    for rows in row_steps(hidden_ref.shape[0]):
        heads = [mixed_ref[head, rows, :] for head in range(QUERY_HEADS)]
        blank = jnp.zeros_like(heads[0])
        first = jnp.concatenate([blank, blank] + join_heads(heads[:5]), axis=1)
        pairs = [other_half(heads[at]) + heads[at + 1] for at in range(5, QUERY_HEADS, 2)]
        last = jnp.concatenate(pairs, axis=1)
        first_ref[rows, :] = first
        last_ref[rows, :] = last
        mid = hidden_ref[rows, :] + mm(first, weights_ref[0], NT) + mm(last, weights_ref[1], NT)
        mid_ref[rows, :] = mid
        normed_ref[rows, :] = (mid * row_scale(mid, width) * gain_ref[...]).astype(BF)


def out_forward(mixed, weights, layer, hidden, gain, width, after=()):
    rows = hidden.shape[0]
    return call(
        functools.partial(out_forward_kernel, width),
        (1,),
        [
            full(QUERY_HEADS, rows, 128),
            pl.BlockSpec((2, WIDE, 640), lambda i: (1, 0, layer)),
            full(rows, WIDE),
            full(1, WIDE),
        ],
        [full(rows, 640), full(rows, 640), full(rows, WIDE), full(rows, WIDE)],
        [
            jax.ShapeDtypeStruct((rows, 640), BF),
            jax.ShapeDtypeStruct((rows, 640), BF),
            jax.ShapeDtypeStruct((rows, WIDE), F32),
            jax.ShapeDtypeStruct((rows, WIDE), BF),
        ],
        [],
        4 * rows * WIDE * 640,
        WIDE * 640 * 4 + rows * WIDE * 10 + rows * 6400,
        (mixed, weights, hidden, gain),
        after,
    )


def norm_back(gradient, hidden, gain, width):
    scaling = row_scale(hidden, width)
    normed = hidden * scaling
    weighted = gradient * gain
    inner = jnp.sum(weighted * normed, axis=-1, keepdims=True) / width
    gain_grad = jnp.sum(gradient * normed, axis=0, keepdims=True)
    return scaling * (weighted - normed * inner), gain_grad


def out_backward_kernel(
    width, back_ref, mid_ref, grad_ref, gain_ref, weights_ref, mid_g, rounded_ref, mixed_g, gain_g
):
    gain_g[...] = jnp.zeros_like(gain_g)
    for rows in row_steps(mid_ref.shape[0]):
        change, gain_part = norm_back(back_ref[rows, :], mid_ref[rows, :], gain_ref[...], width)
        gain_g[...] += gain_part
        change += grad_ref[rows, :]
        mid_g[rows, :] = change
        rounded = change.astype(BF)
        rounded_ref[rows, :] = rounded
        for part in range(2):
            block = mm(rounded, weights_ref[part]).astype(BF)
            for at in range(5):
                for side in range(2):
                    head = part * 10 + at * 2 + side - 5
                    if head >= 0:
                        two = block[:, at * 128 : at * 128 + 128]
                        mixed_g[head, rows, :] = high_lanes(two if side else other_half(two))


def out_backward(back, mid, grad, gain, weights, layer, width, after=()):
    rows = mid.shape[0]
    return call(
        functools.partial(out_backward_kernel, width),
        (1,),
        [
            full(rows, WIDE),
            full(rows, WIDE),
            full(rows, WIDE),
            full(1, WIDE),
            pl.BlockSpec((2, WIDE, 640), lambda i: (1, 0, layer)),
        ],
        [full(rows, WIDE), full(rows, WIDE), full(QUERY_HEADS, rows, 128), full(1, WIDE)],
        [
            jax.ShapeDtypeStruct((rows, WIDE), F32),
            jax.ShapeDtypeStruct((rows, WIDE), BF),
            jax.ShapeDtypeStruct((QUERY_HEADS, rows, 128), BF),
            jax.ShapeDtypeStruct((1, WIDE), F32),
        ],
        [],
        4 * rows * WIDE * 640,
        WIDE * 640 * 4 + rows * WIDE * 18 + rows * 3840,
        (back, mid, grad, gain, weights),
        after,
    )


def query_backward_kernel(
    query_g, normed_ref, rounded_ref, mixed_ref, last_ref, weights_ref, back_ref, out_w, mixed_w, first
):
    for rows in row_steps(normed_ref.shape[0]):
        part = jnp.concatenate(
            [query_g[at, rows, :] + other_half(query_g[at + 1, rows, :]) for at in range(0, 10, 2)], axis=1
        )
        first[rows, :] = part
        back_ref[rows, :] = mm(part, weights_ref[0], NT)
    for at in range(0, WIDE, 256):
        part = pl.ds(at, 256)
        out_w[0, part, :] = mm(normed_ref[:, part], first[...], TN).astype(BF)
        rounded = rounded_ref[:, part]
        out_w[1, part, :] = mm(rounded, last_ref[...], TN).astype(BF)
        mixed_w[part, :] = mm(rounded, mixed_ref[...], TN)


def query_backward(query_g, normed, rounded, mixed, last, weights, layer, after=()):
    rows = normed.shape[0]
    return call(
        query_backward_kernel,
        (1,),
        [
            full(10, rows, 128),
            full(rows, WIDE),
            full(rows, WIDE),
            full(rows, 640),
            full(rows, 640),
            pl.BlockSpec((1, WIDE, 640), lambda i: (0, 0, layer)),
        ],
        [full(rows, WIDE), full(2, WIDE, 640), full(WIDE, 640)],
        [
            jax.ShapeDtypeStruct((rows, WIDE), F32),
            jax.ShapeDtypeStruct((2, WIDE, 640), BF),
            jax.ShapeDtypeStruct((WIDE, 640), F32),
        ],
        [pltpu.VMEM((rows, 640), BF)],
        8 * rows * WIDE * 640,
        WIDE * 640 * 10 + rows * WIDE * 8 + rows * 5120,
        (query_g, normed, rounded, mixed, last, weights),
        after,
    )


def key_backward_kernel(width, shares, *refs):
    pairs = refs[:shares]
    query_g, back_ref, mixed_w, normed_ref, weights_ref, hidden_ref, mid_g, gain_ref = refs[shares : shares + 8]
    cos_ref, sin_ref, grad_ref, rounded_ref, out_w, gain_g, second, third = refs[shares + 8 :]
    gain_g[...] = jnp.zeros_like(gain_g)
    for rows in row_steps(hidden_ref.shape[0]):
        keys, values = [], []
        for group in range(KEY_VALUE_HEADS):
            pair = pairs[0][group, rows, :]
            for other in pairs[1:]:
                pair = pair + other[group, rows, :].astype(F32)
            moved = pair * sin_ref[rows, :]
            lane = lax.broadcasted_iota(jnp.int32, pair.shape, 1)
            turned = jnp.where(lane < HEAD_DIM // 2, pltpu.roll(moved, 96, 1), -pltpu.roll(moved, 32, 1))
            key = pair * cos_ref[rows, :] + turned
            keys.append(low_lanes(key).astype(BF))
            values.append(high_lanes(pair).astype(BF))
        heads = [query_g[at, rows, :] for at in range(5)] + keys
        second_part = jnp.concatenate(
            [heads[at] + other_half(heads[at + 1]) for at in range(0, 10, 2)], axis=1
        )
        third_part = jnp.concatenate(
            [other_half(values[0]) + values[1], other_half(values[2]) + values[3], other_half(values[4])],
            axis=1,
        )
        second[rows, :] = second_part
        third[rows, :] = third_part
        back = (
            back_ref[rows, :]
            + mm(second_part, weights_ref[1], NT)
            + mm(third_part, weights_ref[2, :, :384], NT)
        )
        change, gain_part = norm_back(back, hidden_ref[rows, :], gain_ref[...], width)
        gain_g[...] += gain_part
        grad = mid_g[rows, :] + change
        grad_ref[rows, :] = grad
        rounded_ref[rows, :] = grad.astype(BF)
    for at in range(0, WIDE, 256):
        part = pl.ds(at, 256)
        normed = normed_ref[:, part]
        out_w[0, part, :] = mm(normed, second[...], TN).astype(BF)
        out_w[1, part, :384] = (mm(normed, third[...], TN) + mixed_w[part, :384]).astype(BF)
        out_w[1, part, 384:] = mixed_w[part, 384:].astype(BF)


def key_backward(
    pair_g, arrived, query_g, back, mixed_w, normed, weights, layer, hidden, mid_g, gain, cosine, sine, width, after=()
):
    rows = hidden.shape[0]
    own = pl.BlockSpec((KEY_VALUE_HEADS, rows, 128), lambda i: (0, 0, 0))
    return call(
        functools.partial(key_backward_kernel, width, 1 + len(arrived)),
        (1,),
        [own] * (1 + len(arrived))
        + [
            pl.BlockSpec((5, rows, 128), lambda i: (2, 0, 0)),
            full(rows, WIDE),
            full(WIDE, 640),
            full(rows, WIDE),
            pl.BlockSpec((3, WIDE, 640), lambda i: (0, 0, layer)),
            full(rows, WIDE),
            full(rows, WIDE),
            full(1, WIDE),
            full(rows, 128),
            full(rows, 128),
        ],
        [full(rows, WIDE), full(rows, WIDE), full(2, WIDE, 640), full(1, WIDE)],
        [
            jax.ShapeDtypeStruct((rows, WIDE), F32),
            jax.ShapeDtypeStruct((rows, WIDE), BF),
            jax.ShapeDtypeStruct((2, WIDE, 640), BF),
            jax.ShapeDtypeStruct((1, WIDE), F32),
        ],
        [pltpu.VMEM((rows, 640), BF), pltpu.VMEM((rows, 384), BF)],
        7 * rows * WIDE * 640,
        WIDE * 640 * 12 + rows * WIDE * 20 + rows * 12800,
        (pair_g, *arrived, query_g, back, mixed_w, normed, weights, hidden, mid_g, gain, cosine, sine),
        after,
    )


def diagonal_bias(span):
    key_at = lax.broadcasted_iota(jnp.int32, (span, span), 0)
    query_at = lax.broadcasted_iota(jnp.int32, (span, span), 1)
    return jnp.concatenate([jnp.where(key_at <= query_at, 0.0, MASKED)] * GROUP, axis=1)


def turn_rows(pair_ref, turned, lanes):
    span = pair_ref.shape[1] // 2
    for at in range(0, pair_ref.shape[1], span):
        turned[:, at : at + span] = pair_ref[0, at : at + span, :].astype(F32).T[lanes, :].astype(BF)


def attend_more(query, pair_ref, turned, at, top, norm, mixed):
    more = mm(pair_ref[0, at, :], query, NT) * (SCALE * LOG2E)
    old = top[...]
    peak = jnp.maximum(old, jnp.max(more, axis=0, keepdims=True))
    keep = jnp.exp2(old - peak)
    weight = jnp.exp2(more - peak)
    top[...] = peak
    norm[...] = norm[...] * keep + jnp.sum(weight, axis=0, keepdims=True)
    mixed[...] = mixed[...] * keep + mm(turned[:, at], weight.astype(BF))


def attend_own_kernel(ids_ref, query_ref, pair_ref, top_ref, norm_ref, mixed_ref, turned):
    span = query_ref.shape[1] // 2
    width = GROUP * span
    turn_rows(pair_ref, turned, slice(HEAD_DIM, 2 * HEAD_DIM))
    bias = diagonal_bias(span)
    for s in range(2):
        own, other = slice(s * span, (s + 1) * span), slice((1 - s) * span, (2 - s) * span)
        query = query_ref[:, own, :].reshape(width, 128)
        first = mm(pair_ref[0, own, :], query, NT) * (SCALE * LOG2E) + bias
        peak = jnp.max(first, axis=0, keepdims=True)
        weight = jnp.exp2(first - peak)
        top_ref[0, s] = peak
        norm_ref[0, s] = jnp.sum(weight, axis=0, keepdims=True)
        mixed_ref[0, s] = mm(turned[:, own], weight.astype(BF))

        @pl.when(ids_ref[1 - s] < ids_ref[s])
        def _():
            attend_more(query, pair_ref, turned, other, top_ref.at[0, s], norm_ref.at[0, s], mixed_ref.at[0, s])


def attend_far_kernel(
    ids_ref, query_ref, pair_ref, top_ref, norm_ref, mixed_ref, out_ref, total_ref, turned, top, norm, mixed
):
    span = query_ref.shape[1] // 2
    width = GROUP * span
    turn_rows(pair_ref, turned, slice(HEAD_DIM, 2 * HEAD_DIM))
    for s in range(2):
        own = slice(s * span, (s + 1) * span)
        query = query_ref[:, own, :].reshape(width, 128)
        top[...] = top_ref[0, s]
        norm[...] = norm_ref[0, s]
        mixed[...] = mixed_ref[0, s]
        for j in range(pair_ref.shape[1] // span):

            @pl.when(ids_ref[2 + j] < ids_ref[s])
            def _():
                attend_more(query, pair_ref, turned, slice(j * span, (j + 1) * span), top, norm, mixed)

        total_ref[0, s] = top[...] + jnp.log2(norm[...])
        result = mixed[...] / norm[...]
        result = jnp.concatenate([jnp.zeros_like(result), result], axis=0).T.astype(BF)
        out_ref[:, own, :] = result.reshape(GROUP, span, 128)


def group_specs(rows, keys):
    width = GROUP * rows // 2
    return (
        pl.BlockSpec((GROUP, rows, 128), lambda g, ids: (g, 0, 0)),
        pl.BlockSpec((1, keys, 128), lambda g, ids: (g, 0, 0)),
        pl.BlockSpec((1, 2, 1, width), lambda g, ids: (g, 0, 0, 0)),
        pl.BlockSpec((1, 2, HEAD_DIM, width), lambda g, ids: (g, 0, 0, 0)),
    )


def attend(ids, query, pair, far):
    rows = query.shape[1]
    keys = far.shape[1]
    width = GROUP * rows // 2
    line = jax.ShapeDtypeStruct((KEY_VALUE_HEADS, 2, 1, width), F32)
    block = jax.ShapeDtypeStruct((KEY_VALUE_HEADS, 2, HEAD_DIM, width), F32)
    heads, near, lines, blocks = group_specs(rows, rows)
    *state, _ = call(
        attend_own_kernel,
        (KEY_VALUE_HEADS,),
        [heads, near],
        [lines, lines, blocks],
        [line, line, block],
        [pltpu.VMEM((HEAD_DIM, rows), BF)],
        8 * QUERY_HEADS * rows * rows * 128,
        QUERY_HEADS * rows * 1024,
        (query, pair),
        (),
        (ids,),
    )
    heads, there, lines, blocks = group_specs(rows, keys)
    return call(
        attend_far_kernel,
        (KEY_VALUE_HEADS,),
        [heads, there, lines, lines, blocks],
        [heads, lines],
        [jax.ShapeDtypeStruct((QUERY_HEADS, rows, 128), BF), line],
        [
            pltpu.VMEM((HEAD_DIM, keys), BF),
            pltpu.VMEM((1, width), F32),
            pltpu.VMEM((1, width), F32),
            pltpu.VMEM((HEAD_DIM, width), F32),
        ],
        8 * QUERY_HEADS * rows * keys * 128,
        QUERY_HEADS * rows * 1536,
        (query, far, *state),
        (),
        (ids,),
    )


def attend_back_block(pair_ref, at, query, grad, total, deltas, turned, bias, pair_g):
    pair = pair_ref[0, at, :]
    scores = mm(pair, query, NT) * (SCALE * LOG2E) - total
    if bias is not None:
        scores = scores + bias
    weight = jnp.exp2(scores)
    change = (weight * (mm(pair, grad, NT) - deltas[...])).astype(BF)
    pair_g[at, :] += mm(change, query) * SCALE + mm(weight.astype(BF), grad)
    return mm(turned[:, at], change)


def row_products(grad_ref, out_ref, own, width):
    product = grad_ref[:, own, :].astype(F32) * out_ref[:, own, :].astype(F32)
    return jnp.sum(product.reshape(width, 128).T, axis=0, keepdims=True)


def attend_back_far_kernel(
    ids_ref, query_ref, pair_ref, grad_ref, out_ref, total_ref, mixed_ref, pair_out, turned, deltas, pair_g
):
    span = query_ref.shape[1] // 2
    width = GROUP * span
    turn_rows(pair_ref, turned, slice(0, HEAD_DIM))
    pair_g[...] = jnp.zeros_like(pair_g)
    mixed_ref[...] = jnp.zeros_like(mixed_ref)
    for s in range(2):
        own = slice(s * span, (s + 1) * span)
        query = query_ref[:, own, :].reshape(width, 128)
        grad = grad_ref[:, own, :].reshape(width, 128)
        deltas[...] = row_products(grad_ref, out_ref, own, width)
        for j in range(pair_ref.shape[1] // span):

            @pl.when(ids_ref[2 + j] < ids_ref[s])
            def _():
                at = slice(j * span, (j + 1) * span)
                mixed_ref[0, s] += attend_back_block(
                    pair_ref, at, query, grad, total_ref[0, s], deltas, turned, None, pair_g
                )

    pair_out[0] = pair_g[...].astype(BF)


def attend_back_own_kernel(
    ids_ref,
    query_ref,
    pair_ref,
    grad_ref,
    out_ref,
    total_ref,
    mixed_ref,
    cos_ref,
    sin_ref,
    query_g,
    pair_out,
    turned,
    deltas,
    mixed,
    pair_g,
):
    span = query_ref.shape[1] // 2
    width = GROUP * span
    half = HEAD_DIM // 2
    turn_rows(pair_ref, turned, slice(0, HEAD_DIM))
    pair_g[...] = jnp.zeros_like(pair_g)
    bias = diagonal_bias(span)
    for s in range(2):
        own, other = slice(s * span, (s + 1) * span), slice((1 - s) * span, (2 - s) * span)
        query = query_ref[:, own, :].reshape(width, 128)
        grad = grad_ref[:, own, :].reshape(width, 128)
        deltas[...] = row_products(grad_ref, out_ref, own, width)
        total = total_ref[0, s]
        mixed[...] = mixed_ref[0, s] + attend_back_block(
            pair_ref, own, query, grad, total, deltas, turned, bias, pair_g
        )

        @pl.when(ids_ref[1 - s] < ids_ref[s])
        def _():
            mixed[...] += attend_back_block(
                pair_ref, other, query, grad, total_ref[0, s], deltas, turned, None, pair_g
            )

        cosine = jnp.concatenate([cos_ref[:, own]] * GROUP, axis=1)
        sine = jnp.concatenate([sin_ref[:, own]] * GROUP, axis=1)
        change = mixed[...] * SCALE
        moved = change * sine
        change = change * cosine + jnp.concatenate([moved[half:], -moved[:half]], axis=0)
        change = jnp.concatenate([change, jnp.zeros_like(change)], axis=0).T.astype(BF)
        query_g[:, own, :] = change.reshape(GROUP, span, 128)
    pair_out[0] = pair_g[...]


def attend_back_far(ids, query, far, grad, out, total):
    rows = query.shape[1]
    keys = far.shape[1]
    width = GROUP * rows // 2
    heads, there, lines, blocks = group_specs(rows, keys)
    return call(
        attend_back_far_kernel,
        (KEY_VALUE_HEADS,),
        [heads, there, heads, heads, lines],
        [blocks, there],
        [
            jax.ShapeDtypeStruct((KEY_VALUE_HEADS, 2, HEAD_DIM, width), F32),
            jax.ShapeDtypeStruct((KEY_VALUE_HEADS, keys, 128), BF),
        ],
        [pltpu.VMEM((HEAD_DIM, keys), BF), pltpu.VMEM((1, width), F32), pltpu.VMEM((keys, 128), F32)],
        20 * QUERY_HEADS * rows * keys * 128,
        QUERY_HEADS * rows * 2048,
        (query, far, grad, out, total),
        (),
        (ids,),
    )


def attend_back_own(ids, query, pair, grad, out, total, mixed, cosine_t, sine_t):
    rows = query.shape[1]
    width = GROUP * rows // 2
    heads, near, lines, blocks = group_specs(rows, rows)
    return call(
        attend_back_own_kernel,
        (KEY_VALUE_HEADS,),
        [heads, near, heads, heads, lines, blocks, full(HEAD_DIM, rows), full(HEAD_DIM, rows)],
        [heads, near],
        [
            jax.ShapeDtypeStruct((QUERY_HEADS, rows, 128), BF),
            jax.ShapeDtypeStruct((KEY_VALUE_HEADS, rows, 128), F32),
        ],
        [
            pltpu.VMEM((HEAD_DIM, rows), BF),
            pltpu.VMEM((1, width), F32),
            pltpu.VMEM((HEAD_DIM, width), F32),
            pltpu.VMEM((rows, 128), F32),
        ],
        20 * QUERY_HEADS * rows * rows * 128,
        QUERY_HEADS * rows * 2560,
        (query, pair, grad, out, total, mixed, cosine_t, sine_t),
        (),
        (ids,),
    )


def plain_scores(query, pairs, places, own):
    grouped = query[..., :HEAD_DIM].reshape(KEY_VALUE_HEADS, GROUP, -1, HEAD_DIM)
    scores = jnp.einsum("kgqd,ktd->kgqt", grouped, pairs[..., :HEAD_DIM], preferred_element_type=F32)
    return grouped, jnp.where(places[None, :] <= own[:, None], scores * SCALE, MASKED)


def plain_attend(places, query, pair, far):
    rows = query.shape[1]
    pairs = jnp.concatenate([pair, far], axis=1)
    _, scores = plain_scores(query, pairs, places, places[:rows])
    top = jnp.max(scores, axis=-1, keepdims=True)
    weight = jnp.exp(scores - top)
    norm = jnp.sum(weight, axis=-1, keepdims=True)
    mixed = jnp.einsum(
        "kgqt,ktd->kgqd", (weight / norm).astype(BF), pairs[..., HEAD_DIM:], preferred_element_type=F32
    )
    mixed = jnp.pad(mixed.reshape(QUERY_HEADS, rows, HEAD_DIM), ((0, 0), (0, 0), (HEAD_DIM, 0)))
    return mixed.astype(BF), top + jnp.log(norm), jnp.zeros((1,), jnp.int32)


def plain_attend_back(places, query, pairs, grad, out, total, cosine_t, sine_t, after=()):
    rows = query.shape[1]
    half = HEAD_DIM // 2
    grouped, scores = plain_scores(query, pairs, places, places[:rows])
    weight = jnp.exp(scores - total)
    grad = grad[..., HEAD_DIM:].reshape(grouped.shape)
    reach = jnp.einsum("kgqd,ktd->kgqt", grad, pairs[..., HEAD_DIM:], preferred_element_type=F32)
    change = (weight * (reach - jnp.sum(weight * reach, axis=-1, keepdims=True))).astype(BF)
    query_g = SCALE * jnp.einsum("kgqt,ktd->kgqd", change, pairs[..., :HEAD_DIM], preferred_element_type=F32)
    key_g = SCALE * jnp.einsum("kgqt,kgqd->ktd", change, grouped, preferred_element_type=F32)
    value_g = jnp.einsum("kgqt,kgqd->ktd", weight.astype(BF), grad, preferred_element_type=F32)
    moved = query_g * sine_t.T
    query_g = query_g * cosine_t.T + jnp.concatenate([moved[..., half:], -moved[..., :half]], axis=-1)
    query_g = jnp.pad(query_g.reshape(QUERY_HEADS, rows, HEAD_DIM), ((0, 0), (0, 0), (0, HEAD_DIM)))
    return query_g.astype(BF), jnp.concatenate([key_g, value_g], axis=-1), jnp.zeros((1,), jnp.int32)


def local(
    tokens,
    span_ids,
    w_query,
    key_weight,
    value_weight,
    w_out,
    gain_attn,
    gain_mlp,
    w_gate,
    w_up,
    w_down,
    out_grad,
):
    group_count, local_length, model_width = tokens.shape
    assert group_count == 1
    n_ctx = lax.axis_size("ctx")
    n_shard = lax.axis_size("shard")
    blocks = n_ctx * n_shard
    own_rows = model_width // blocks
    rows = WIDE // blocks
    extra = rows - own_rows
    tp_rank = lax.axis_index("tp")
    ctx_rank = lax.axis_index("ctx")
    span = local_length // 2

    ids = jnp.concatenate(
        [lax.dynamic_slice_in_dim(span_ids, 2 * ((ctx_rank - i) % n_ctx), 2) for i in range(n_ctx)]
    )
    places = (ids[:, None] * span + jnp.arange(span, dtype=jnp.int32)[None, :]).reshape(-1)
    own_place = places[:local_length].astype(F32)
    inverse_freq = THETA ** (-jnp.arange(HEAD_DIM // 2, dtype=F32) * 2.0 / HEAD_DIM)
    angles = own_place[:, None] * jnp.tile(inverse_freq, 4)[None, :]
    cosine, sine = jnp.cos(angles), jnp.sin(angles)
    angles_t = jnp.tile(inverse_freq, 2)[:, None] * own_place[None, :]
    cosine_t, sine_t = jnp.cos(angles_t), jnp.sin(angles_t)

    source = jnp.arange(model_width, dtype=jnp.int32)
    target = source // own_rows * rows + source % own_rows
    spread = (target[:, None] == jnp.arange(WIDE, dtype=jnp.int32)[None, :]).astype(BF)

    def attn_share(layer):
        joined = jnp.concatenate(
            [w_query[layer], key_weight[layer], value_weight[layer], w_out[layer].T], axis=1
        )
        gains = jnp.concatenate(
            [
                jnp.pad(gain_attn[layer], (0, 128 - own_rows)),
                jnp.pad(gain_mlp[layer], (0, 2560 - 128 - own_rows)),
            ]
        )
        joined = jnp.concatenate([joined, gains[None, :], jnp.zeros((extra - 1, 2560), BF)], axis=0)
        return lax.dynamic_slice_in_dim(joined, tp_rank * 640, 640, 1)

    def mlp_share(layer):
        joined = jnp.concatenate([w_gate[layer], w_up[layer], w_down[layer].T], axis=1)
        return jnp.pad(joined, ((0, extra), (0, 0)))

    def gather(share):
        return lax.all_gather(share, ("tp", "shard", "ctx"), axis=0, tiled=True).reshape(
            4, WIDE, share.shape[1]
        )


    def gains_of(weights, layer):
        lines = weights[0, :, layer * 640 : layer * 640 + 640].reshape(blocks, rows, 640)[:, own_rows, :]
        return tuple(
            lines[:, at : at + rows].reshape(WIDE).astype(F32)[None, :] for at in (0, 128)
        )

    use_kernels = span % 128 == 0
    if use_kernels:
        attend_call = functools.partial(attend, ids)
    else:
        attend_call = functools.partial(plain_attend, places)

    columns = w_gate.shape[2]
    shares = [attn_share(layer) for layer in range(DECODER_LAYERS)]
    front_w = gather(jnp.concatenate([*shares, mlp_share(0)], axis=1))
    mlp_w = [(front_w, DECODER_LAYERS)]
    for layer in range(1, DECODER_LAYERS):
        mlp_w.append((gather(mlp_share(layer)), 0))

    hidden = mm(tokens[0], spread)
    kept = []
    for layer in range(DECODER_LAYERS):
        weights = front_w
        gain_a, gain_m = gains_of(weights, layer)
        attn_in, query, pair, _ = project(hidden, gain_a, weights, layer, cosine, sine, model_width)
        far = [
            lax.ppermute(pair, "ctx", [(i, (i + shift) % n_ctx) for i in range(n_ctx)])
            for shift in range(1, n_ctx)
        ]
        far = far[0] if n_ctx == 2 else jnp.concatenate(far, axis=1)
        mixed, total, _ = attend_call(query, pair, far)
        first, last, mid, mlp_in, _ = out_forward(mixed, weights, layer, hidden, gain_m, model_width)
        result, gate, up, _ = mlp_forward(mlp_in, mid, *mlp_w[layer], columns)
        kept.append(
            (hidden, weights, gain_a, gain_m, attn_in, query, pair, far, mixed, total, first, last, mid, mlp_in, gate, up)
        )
        hidden = result
    block_out = mm(hidden.astype(BF), spread, NT).astype(BF)[None]

    core = tp_rank % 2
    grad_run = mm(out_grad[0], spread)
    grad_in = grad_run.astype(BF)
    blank = jnp.zeros_like(grad_run)
    mlp_done, attn_done = [None] * DECODER_LAYERS, [None] * DECODER_LAYERS
    for layer in reversed(range(DECODER_LAYERS)):
        (hidden, weights, gain_a, gain_m, attn_in, query, pair, far, mixed, total, first, last, mid, mlp_in, gate, up) = kept[layer]
        sources = (gate, up, *mlp_w[layer])
        final = layer == 0
        ready = ()
        if final:
            ready = tips(attn_sum.advance()[:2])
        order = jnp.arange(4, dtype=jnp.int32)
        back, parts, token = mlp_backward(order, 1, grad_in, mlp_in, blank, *sources)
        mlp_done[layer] = lax.psum_scatter(
            parts.reshape(4 * WIDE, -1), ("tp", "shard", "ctx"), scatter_dimension=0, tiled=True
        )
        mid_g, rounded, mixed_g, gain_m_grad, _ = out_backward(
            back, mid, grad_run, gain_m, weights, layer, model_width, after=ready
        )
        ready = ()
        if final:
            ready = tips(attn_sum.advance(token[0]))
        if use_kernels:
            part, far_g, _ = attend_back_far(ids, query, far, mixed_g, mixed, total)
        else:
            query_g, pair_g, token = plain_attend_back(
                places, query, jnp.concatenate([pair, far], axis=1), mixed_g, mixed, total, cosine_t, sine_t
            )
            pair_g, far_g = pair_g[:, :local_length], pair_g[:, local_length:].astype(BF)
        arrived = [
            lax.ppermute(
                far_g[:, (shift - 1) * local_length : shift * local_length] if n_ctx > 2 else far_g,
                "ctx",
                [(i, (i - shift) % n_ctx) for i in range(n_ctx)],
            )
            for shift in range(1, n_ctx)
        ]
        if use_kernels:
            query_g, pair_g, token = attend_back_own(
                ids, query, pair, mixed_g, mixed, total, part, cosine_t, sine_t
            )
        if final:
            attn_sum.advance(token[0])
            ready = ready + tips(mlp_done[layer + 1 :])
        back, early, mixed_w, token = query_backward(
            query_g, attn_in, rounded, first, last, weights, layer, after=ready
        )
        grad_run, grad_in, late, gain_a_grad, token = key_backward(
            pair_g,
            arrived,
            query_g,
            back,
            mixed_w,
            attn_in,
            weights,
            layer,
            hidden,
            mid_g,
            gain_a,
            cosine,
            sine,
            model_width,
        )
        if final:
            attn_done[layer + 1] = attn_sum.advance(token[0])[0]
        lines = jnp.concatenate(
            [
                jnp.pad(gain_a_grad.reshape(blocks, rows), ((0, 0), (0, 128 - rows))),
                jnp.pad(gain_m_grad.reshape(blocks, rows), ((0, 0), (0, 640 - 128 - rows))),
            ],
            axis=1,
        ).astype(BF)
        at = lax.broadcasted_iota(jnp.int32, (1, rows, 1), 1)
        second_w = jnp.where(at == own_rows, lines[:, None, :], late[0].reshape(blocks, rows, 640))
        second_w = second_w.reshape(WIDE, 640)
        there, here = [], []
        for part in (slice(0, WIDE // 2), slice(WIDE // 2, WIDE)):
            parts = early[0, part], second_w[part], late[1, part], early[1, part]
            there.append(
                jnp.stack([jnp.where(core == 0, parts[1], parts[0]), jnp.where(core == 0, parts[3], parts[2])])
            )
            here.append(
                jnp.stack([jnp.where(core == 0, parts[0], parts[1]), jnp.where(core == 0, parts[2], parts[3])])
            )
        attn_sum = Reduction(there, here, n_shard, n_ctx, rows)
    for _ in range(4):
        attn_sum.advance()
    attn_done[0] = attn_sum.values[0]
    attn_done = gather_core(gather_pair(jnp.stack(attn_done)), 1)

    grad_high = grad_run.astype(BF)
    grad_low = (grad_run - grad_high.astype(F32)).astype(BF)
    tokens_grad = (mm(grad_high, spread, NT) + mm(grad_low, spread, NT))[None]

    outs = [[] for _ in range(9)]
    for layer, mlp in enumerate(mlp_done):
        attn = attn_done[:, :, layer].reshape(4, rows, 640)
        line = attn[1, own_rows].astype(F32)
        attn = attn[:, :own_rows].transpose(1, 0, 2).reshape(own_rows, 2560).astype(F32)
        mlp = mlp[:own_rows].astype(F32)
        columns = mlp.shape[1] // 3
        for slot, value in enumerate(
            (
                attn[:, :960],
                attn[:, 960:1280],
                attn[:, 1280:1600],
                attn[:, 1600:].T,
                line[:own_rows],
                line[128 : 128 + own_rows],
                mlp[:, :columns],
                mlp[:, columns : 2 * columns],
                mlp[:, 2 * columns :].T,
            )
        ):
            outs[slot].append(value)
    return (block_out, tokens_grad, *[jnp.stack(parts) for parts in outs])


def solution(mesh):
    return jax.shard_map(
        local,
        mesh=mesh,
        in_specs=(
            P(("shard", "tp"), "ctx", None),
            P(),
            P(None, ("shard", "ctx"), None),
            P(None, ("shard", "ctx"), None),
            P(None, ("shard", "ctx"), None),
            P(None, None, ("shard", "ctx")),
            P(None, ("shard", "ctx")),
            P(None, ("shard", "ctx")),
            P(None, ("shard", "ctx"), "tp"),
            P(None, ("shard", "ctx"), "tp"),
            P(None, "tp", ("shard", "ctx")),
            P(("shard", "tp"), "ctx", None),
        ),
        out_specs=(
            P(("shard", "tp"), "ctx", None),
            P(("shard", "tp"), "ctx", None),
            P(None, ("shard", "ctx"), None),
            P(None, ("shard", "ctx"), None),
            P(None, ("shard", "ctx"), None),
            P(None, None, ("shard", "ctx")),
            P(None, ("shard", "ctx")),
            P(None, ("shard", "ctx")),
            P(None, ("shard", "ctx"), "tp"),
            P(None, ("shard", "ctx"), "tp"),
            P(None, "tp", ("shard", "ctx")),
        ),
        check_vma=False,
    )
```
